128 devices in a mesh: ctx: 32 (over z, x, core), win: 4 (over y).
Axes of the slice: x: 4, y: 4, z: 4, core: 2. Of those that a mesh axis runs over, the one named last changes fastest.
Arguments:
- hidden: bfloat16 [4, 32768, 7168], P('win', 'ctx')
- router_weight: bfloat16 [7168, 256], replicated
- expert_ids: int32 [4, 32768, 8], P('win', 'ctx'), may hold values from 0 to 255, as said below
- doc_lengths: int32 [4, 64], P('win'), may hold values from 1 to 8192, 32768 in all within a row
Outputs:
- balance: float32 [4], P('win')
- logit_grad: float32 [4, 32768, 256], P('win', 'ctx')
- weight_grad: float32 [7168, 256], P(('ctx', 'win'))
The draws below stay inside these ranges and needn't reach their ends.
Inputs may be any that keep to these rules, and one draw needn't show every extreme that they name: Each window's document lengths are at least 1, sum to 32768, and the largest is exactly 8192; documents follow one another in the order of doc_lengths. `expert_ids`: each token names 8 different experts.
All inputs are finite; a program needn't handle non-finite values.
Results may differ from the reference program's by a relative error of at most 0.0026.
Values sent between devices are 32-bit elements; how exact they have to be, the bound alone decides.
A program may use at most 128 MiB of HBM per device.

```python
import math
import jax
import jax.numpy as jnp
import numpy as np
from jax import lax

D = 7168
E = 256
K = 8
TOK_DEV = 1024
DOCS = 64
WINDOWS = 4
LENGTH = 32768
MOST_DOC = 8192


def common_weight(key):
    weight_key = jax.random.fold_in(key, 101)
    values = jnp.clip(jax.random.normal(weight_key, (D, E), jnp.float32), -6.0, 6.0)
    return (values * (1.0 / math.sqrt(D))).astype(jnp.bfloat16)


def common_choices(key):
    pick_key = jax.random.fold_in(key, 202)
    blocks = LENGTH // TOK_DEV
    popular = jax.random.randint(jax.random.fold_in(pick_key, 1), (WINDOWS, blocks, 1, E), 0, 4, dtype=jnp.int32)
    jitter = jax.random.randint(jax.random.fold_in(pick_key, 2), (WINDOWS, blocks, TOK_DEV, E), 0, 4096, dtype=jnp.int32)
    scores = (jitter + popular * 128) * E + jnp.arange(E, dtype=jnp.int32)
    ranked, chosen = lax.top_k(scores, K)
    return chosen.reshape(WINDOWS, LENGTH, K).astype(jnp.int32)


def draw_router_weight(key, part):
    return common_weight(key)


def draw_expert_ids(key, part):
    return common_choices(key)


def draw_hidden(key, part):
    chosen = common_choices(key)
    columns = common_weight(key).astype(jnp.float32).T
    key = jax.random.fold_in(key, 3)
    scale_low, scale_high, strength = (1.0, 1.0, 3.0)
    blocks = LENGTH // TOK_DEV
    pieces = blocks * WINDOWS
    width_block = D // pieces
    target = jax.random.permutation(jax.random.fold_in(key, 7), pieces)
    column_block = jnp.arange(D, dtype=jnp.int32) // width_block
    grouped = chosen.reshape(WINDOWS, blocks, TOK_DEV, K)

    def one_block(block_index):
        window = block_index // blocks
        within = block_index % blocks
        picked_ids = grouped[window, within]
        block_key = jax.random.fold_in(key, block_index)
        jitter = jnp.clip(jax.random.normal(block_key, (TOK_DEV, D), jnp.float32), -6.0, 6.0)
        row_scale = jnp.exp(jax.random.uniform(jax.random.fold_in(block_key, 1), (TOK_DEV, 1), jnp.float32, math.log(scale_low), math.log(scale_high)))
        spike_gain = jnp.where(column_block == target[within * WINDOWS + window], 4.0, 1.0).astype(jnp.float32)
        signal = jnp.zeros((TOK_DEV, D), jnp.float32)
        for step in range(K):
            signal = signal + columns[picked_ids[:, step]]
        return (row_scale * (jitter * spike_gain[None, :] + strength * signal)).astype(jnp.bfloat16)
    result = lax.map(one_block, jnp.arange(pieces, dtype=jnp.int32))
    return result.reshape(WINDOWS, LENGTH, D)


def profile(count, total, reach, slope):
    portions = [(1 << 20) // math.isqrt(standing ** slope) + 1 for standing in range(2, count + 1)]
    surplus, given = total - reach - (count - 1), [1] * (count - 1)
    while surplus > 0:
        candidates = [i for i in range(count - 1) if given[i] < reach]
        pool, remaining = sum([portions[i] for i in candidates]), surplus
        for i in candidates:
            more = min(reach - given[i], max(1, remaining * portions[i] // pool), surplus)
            given[i] = given[i] + more
            surplus = surplus - more
    return np.array([reach] + given)


def ragged_sizes(stream_key, count, total, limit, skew):
    if count == 2:
        one = jax.random.randint(stream_key, (), max(1, total - limit), min(limit, total - 1) + 1)
        return jnp.stack([one, total - one])
    tallies = jnp.asarray(profile(count, total, limit, skew), jnp.int32)
    pairs = (count - 1) // 2
    source_of, sink = tallies[1:1 + 2 * pairs:2], tallies[2:2 + 2 * pairs:2]
    margin = jnp.minimum(source_of - 1, limit - sink)
    shifted = jax.random.randint(jax.random.fold_in(stream_key, 1), (pairs,), 0, 1 << 20) % (margin + 1)
    tallies = tallies.at[1:1 + 2 * pairs:2].set(source_of - shifted).at[2:2 + 2 * pairs:2].set(sink + shifted)
    return tallies[jax.random.permutation(jax.random.fold_in(stream_key, 2), count)]


def setup_inputs(seed: int = 0) -> dict:
    streams_of = jax.random.split(jax.random.key(seed), 5)
    return {
        "hidden": draw_hidden(jax.random.fold_in(streams_of[4], 71), 0),
        "router_weight": draw_router_weight(jax.random.fold_in(streams_of[4], 71), 0),
        "expert_ids": draw_expert_ids(jax.random.fold_in(streams_of[4], 71), 0),
        "doc_lengths": jax.vmap(lambda own: ragged_sizes(own, DOCS, LENGTH, MOST_DOC, 2))(jax.random.split(streams_of[3], WINDOWS)).reshape((WINDOWS, DOCS)).astype(jnp.int32),
    }


def reference(hidden, router_weight, expert_ids, doc_lengths):
    weight32 = router_weight.astype(jnp.float32)
    total_grad = jnp.zeros((D, E), jnp.float32)
    balances = []
    grads = []
    for window in range(WINDOWS):
        states = hidden[window].astype(jnp.float32)
        logits = jnp.dot(states, weight32, precision=lax.Precision.HIGHEST)
        affinity = jax.nn.sigmoid(logits)
        total = lax.optimization_barrier(jnp.sum(affinity, axis=-1, keepdims=True))
        share = affinity / total
        picked = lax.optimization_barrier(jnp.sum((expert_ids[window][:, :, None] == jnp.arange(E, dtype=jnp.int32)[None, None, :]).astype(jnp.float32), axis=1))
        chosen_aff = picked * affinity
        pick_gate = chosen_aff / lax.optimization_barrier(jnp.sum(chosen_aff, axis=-1, keepdims=True))
        ends = jnp.cumsum(doc_lengths[window]).astype(jnp.int32)
        position = jnp.arange(LENGTH, dtype=jnp.int32)
        document = lax.optimization_barrier(jnp.sum((ends[None, :] <= position[:, None]).astype(jnp.int32), axis=1))
        member = (document[:, None] == jnp.arange(DOCS, dtype=jnp.int32)[None, :]).astype(jnp.float32)
        counts = jnp.dot(member.T, pick_gate, precision=lax.Precision.HIGHEST)
        shares_sum = jnp.dot(member.T, share, precision=lax.Precision.HIGHEST)
        rates = counts * float(E) / doc_lengths[window].astype(jnp.float32)[:, None]
        balances.append(jnp.sum(rates * shares_sum) / LENGTH)
        token_rates = jnp.dot(member, rates, precision=lax.Precision.HIGHEST)
        centred = token_rates - lax.optimization_barrier(jnp.sum(token_rates * share, axis=-1, keepdims=True))
        grad = E * affinity * (1.0 - affinity) / total * centred
        grads.append(grad)
        rounded = grad.astype(jnp.bfloat16).astype(jnp.float32)
        total_grad = total_grad + jnp.dot(states.T, rounded, precision=lax.Precision.HIGHEST)
    weight_grad = total_grad / math.sqrt(WINDOWS * LENGTH)
    return (jnp.stack(balances), jnp.stack(grads), weight_grad)
```

```python
import functools
import math

import jax
import jax.numpy as jnp
from jax import lax
from jax.experimental import pallas as pl
from jax.experimental.pallas import tpu as pltpu
from jax.sharding import PartitionSpec as P

MESH = pl.DeviceIdType.MESH
F32 = jnp.float32
BF16 = jnp.bfloat16

D, E, K = 7168, 256, 8
TOK = 1024
DOCS = 64
CTX = 32
LENGTH = TOK * CTX
TCH = 256
NTCH = TOK // TCH
ROWS = D // 128
RA = 40
RC = ROWS - RA
CHUNK = 16 * ROWS
OFFS = (2, 1, 3)

PEERS = sorted(
    ((dz, dx, dc) for dz in range(4) for dx in range(4) for dc in range(2) if dz or dx or dc),
    key=lambda o: -(min(o[0], 4 - o[0]) + min(o[1], 4 - o[1]) + o[2]),
)


def split2(v):
    hi = v.astype(BF16)
    lo = (v - hi.astype(F32)).astype(BF16)
    return hi, lo


def dot(a, b):
    return jnp.dot(a, b, preferred_element_type=F32)


def kernel(
    hid, wgt, ids, lens_ref, bal_ref, grad_out, wg_ref,
    xs, ws, picked, share, coef, gbf, dw, crecv,
    pa, pb, pc, ar1, br1, cr1, sa, sb, sc, ar2, br2, cr2, ta, tb, tc, ar3, br3, cr3,
    msg, gat, bmsg, bgat, member2,
    xsem, wsem, osem, gss, grs, bss, brs, css, crs, s1, r1, s2, r2, s3, r3,
):
    ctx = lax.axis_index("ctx")
    y = lax.axis_index("win")
    z, x, c = ctx // 8, (ctx // 2) % 4, ctx % 2

    def at(dz, dx, dc, dy):
        return (((z + dz) % 4 * 4 + (x + dx) % 4) * 2 + (c + dc) % 2, (y + dy) % 4)

    wcopy = pltpu.make_async_copy(wgt, ws, wsem)
    wcopy.start()
    xcopies = []
    for t in range(NTCH):
        cp = pltpu.make_async_copy(hid.at[pl.ds(t * TCH, TCH)], xs.at[pl.ds(t * TCH, TCH)], xsem.at[t])
        cp.start()
        xcopies.append(cp)

    barrier = pltpu.get_barrier_semaphore()
    for dz, dx, dc in PEERS:
        pl.semaphore_signal(barrier, inc=1, device_id=at(dz, dx, dc, 0), device_id_type=MESH)
    for dy in OFFS:
        pl.semaphore_signal(barrier, inc=1, device_id=at(0, 0, 0, dy), device_id_type=MESH)

    lens = jnp.broadcast_to(lens_ref[...].astype(F32), (DOCS, DOCS))
    row = lax.broadcasted_iota(jnp.int32, (DOCS, DOCS), 0)
    col = lax.broadcasted_iota(jnp.int32, (DOCS, DOCS), 1)
    len_c = jnp.sum(jnp.where(row == col, lens, 0.0), axis=1, keepdims=True)
    end_c = jnp.sum(jnp.where(col <= row, lens, 0.0), axis=1, keepdims=True)
    start_c = end_c - len_c
    row2 = lax.broadcasted_iota(jnp.int32, (DOCS, 2 * DOCS), 0)
    col2 = lax.broadcasted_iota(jnp.int32, (DOCS, 2 * DOCS), 1) % DOCS
    end_r = jnp.sum(jnp.where(row2 <= col2, len_c, 0.0), axis=0, keepdims=True)
    start_r = jnp.sum(jnp.where(row2 < col2, len_c, 0.0), axis=0, keepdims=True)
    base = (ctx * TOK).astype(F32)

    def inside(lo, hi, pos):
        return (lo <= pos) & (pos < hi)

    pos_t = lax.broadcasted_iota(jnp.int32, (TOK, 2 * DOCS), 0).astype(F32) + base
    member2[...] = jnp.where(inside(start_r, end_r, pos_t), 1.0, 0.0).astype(BF16)
    sel_first = inside(start_c, end_c, base)
    sel_last = inside(start_c, end_c, base + (TOK - 1))
    gcol = lax.broadcasted_iota(jnp.int32, (2 * DOCS, 8 * CTX), 1)
    grow = lax.broadcasted_iota(jnp.int32, (2 * DOCS, 8 * CTX), 0)
    kind = gcol % 8
    head = ((gcol // 8) * TOK).astype(F32)
    start2 = jnp.concatenate([start_c, start_c], axis=0)
    end2 = jnp.concatenate([end_c, end_c], axis=0)
    half = grow // DOCS
    s_first = (kind == half) & inside(start2, end2, head)
    s_last = (kind == half + 2) & inside(start2, end2, head + (TOK - 1)) & (start2 > head)
    smat = jnp.where(s_first | s_last, 1.0, 0.0).astype(BF16)

    idt = ids[...].astype(F32).T
    lane = lax.broadcasted_iota(jnp.int32, (TCH, E), 1).astype(F32)
    for t in range(NTCH):
        hit = idt[t * TCH : (t + 1) * TCH, 0:1] == lane
        for k in range(1, K):
            hit = hit | (idt[t * TCH : (t + 1) * TCH, k : k + 1] == lane)
        picked[pl.ds(t * TCH, TCH), :] = jnp.where(hit, 1.0, 0.0)

    wcopy.wait()
    local = jnp.zeros((DOCS, 2 * E), F32)
    for t in range(NTCH):
        rows = pl.ds(t * TCH, TCH)
        xcopies[t].wait()
        logits = dot(xs[rows, :], ws[...])
        aff = jax.nn.sigmoid(logits)
        total = jnp.sum(aff, axis=-1, keepdims=True)
        sh = aff * (1.0 / total)
        share[rows, :] = sh
        coef[rows, :] = (float(E) * sh) * (1.0 - aff)
        chosen = picked[rows, :] * aff
        gate = chosen * (1.0 / jnp.sum(chosen, axis=-1, keepdims=True))
        pos = lax.broadcasted_iota(jnp.int32, (DOCS, TCH), 1).astype(F32) + (base + float(t * TCH))
        mem = jnp.where(inside(start_c, end_c, pos), 1.0, 0.0).astype(BF16)
        local = local + dot(mem, jnp.concatenate(split2(gate), axis=1))
    local = local[:, :E] + local[:, E:]

    first = jnp.sum(jnp.where(sel_first, local, 0.0), axis=0, keepdims=True)
    last = jnp.sum(jnp.where(sel_last, local, 0.0), axis=0, keepdims=True)
    tile = jnp.concatenate(
        [first[:, :128], first[:, 128:], last[:, :128], last[:, 128:], jnp.zeros((4, 128), F32)], axis=0
    )
    msg[...] = tile
    gat[pl.ds(ctx, 1)] = tile[None]

    pl.semaphore_wait(barrier, len(PEERS) + len(OFFS))

    def spread(src, dst, ssem, rsem):
        out = []
        for k, (dz, dx, dc) in enumerate(PEERS):
            cp = pltpu.make_async_remote_copy(
                src_ref=src, dst_ref=dst.at[ctx], send_sem=ssem.at[k], recv_sem=rsem.at[k],
                device_id=at(dz, dx, dc, 0), device_id_type=MESH,
            )
            cp.start()
            out.append(cp)
        return out

    gcopies = spread(msg, gat, gss, grs)
    for cp in gcopies:
        cp.wait_recv()
    ghi, glo = split2(gat[...].reshape(8 * CTX, 128))
    sums = dot(smat, jnp.concatenate([ghi, glo], axis=1))
    sums = sums[:, :128] + sums[:, 128:]
    counts = jnp.concatenate([sums[:DOCS], sums[DOCS:]], axis=1)
    counts = counts + jnp.where(sel_first | sel_last, 0.0, local)
    rates = counts * float(E) / len_c
    rates2 = jnp.concatenate(split2(rates), axis=0)

    gsum = jnp.zeros((1, 1), F32)
    for t in range(NTCH):
        rows = pl.ds(t * TCH, TCH)
        tr = dot(member2[rows, :], rates2)
        mean = jnp.sum(tr * share[rows, :], axis=-1, keepdims=True)
        gsum = gsum + jnp.sum(mean, axis=0, keepdims=True)
        g = coef[rows, :] * (tr - mean)
        share[rows, :] = g
        gbf[rows, :] = g.astype(BF16)
    gout = pltpu.make_async_copy(share, grad_out, osem)
    gout.start()

    zq = [(z + o) % 4 for o in OFFS] + [z]
    ccopies, sends = [], []

    def second(i):
        off = pl.multiple_of(zq[i // 2] * (2 * CHUNK) + (i % 2) * CHUNK, 128)
        prod = lax.dot_general(
            xs[:, pl.ds(off, CHUNK)], gbf[...], (((0,), (0,)), ((), ())), preferred_element_type=F32
        )
        dw[i] = prod.reshape(2, 2, 4 * ROWS, E)
        cp = pltpu.make_async_remote_copy(
            src_ref=dw.at[i, :, 1 - c], dst_ref=crecv.at[i], send_sem=css.at[i], recv_sem=crs.at[i],
            device_id=at(0, 0, 1, 0), device_id_type=MESH,
        )
        cp.start()
        ccopies.append(cp)

    def core_sum(i):
        ccopies[i].wait_recv()
        q = i // 2
        for xi in range(2):
            xd = 2 * (i % 2) + xi
            v = (dw[i, xi, pl.ds(c, 1)][0] + crecv[i, xi]).reshape(4, ROWS, E)
            pa[q, xd] = v[:, :RA, :128]
            for yd in range(4):
                pb[q, yd, xd] = v[yd, :RA, 128:]
            pc[q, xd] = v[:, RA:, :]

    def send(src, dst, ssem, rsem, where):
        cp = pltpu.make_async_remote_copy(
            src_ref=src, dst_ref=dst, send_sem=ssem, recv_sem=rsem, device_id=where, device_id_type=MESH
        )
        cp.start()
        sends.append(cp)
        return cp

    got = {}

    def stage1(q):
        for k, o in enumerate(OFFS):
            got["a1", q, k] = send(pa.at[q, (x + o) % 4], ar1.at[q, k], s1.at[0, q, k], r1.at[0, q, k], at(0, o, 0, 0))
            got["b1", q, k] = send(pb.at[q, (y + o) % 4], br1.at[q, k], s1.at[1, q, k], r1.at[1, q, k], at(0, 0, 0, o))
        if q < 3:
            got["c1", q] = send(pc.at[q], cr1.at[q], s1.at[2, q, 0], r1.at[2, q, 0], at(OFFS[q], 0, 0, 0))

    for i in range(9):
        if i < 8:
            second(i)
        if i >= 1:
            core_sum(i - 1)
            if (i - 1) % 2:
                stage1((i - 1) // 2)
        if i == 2:
            btile = jnp.broadcast_to(gsum, (8, 128))
            bmsg[...] = btile
            bgat[pl.ds(ctx, 1)] = btile[None]
            bcopies = spread(bmsg, bgat, bss, brs)

    def stage2a(q):
        for k in range(3):
            got["a1", q, k].wait_recv()
        sa[q] = pa[q, pl.ds(x, 1)][0] + ar1[q, 0] + ar1[q, 1] + ar1[q, 2]
        for k, o in enumerate(OFFS):
            got["a2", q, k] = send(sa.at[q, (y + o) % 4], ar2.at[q, k], s2.at[0, q, k], r2.at[0, q, k], at(0, 0, 0, o))

    def stage2b(q):
        for k in range(3):
            got["b1", q, k].wait_recv()
        sb[q] = pb[q, pl.ds(y, 1)][0] + br1[q, 0] + br1[q, 1] + br1[q, 2]
        if q < 3:
            got["b2", q] = send(sb.at[q], br2.at[q], s2.at[1, q, 0], r2.at[1, q, 0], at(OFFS[q], 0, 0, 0))

    def stage2c():
        for k in range(3):
            got["c1", k].wait_recv()
        sc[...] = pc[3] + cr1[0] + cr1[1] + cr1[2]
        for k, o in enumerate(OFFS):
            got["c2", k] = send(sc.at[(x + o) % 4], cr2.at[k], s2.at[2, 0, k], r2.at[2, 0, k], at(0, o, 0, 0))

    def stage3a(q):
        for k in range(3):
            got["a2", q, k].wait_recv()
        ta[q] = sa[q, pl.ds(y, 1)][0] + ar2[q, 0] + ar2[q, 1] + ar2[q, 2]
        if q < 3:
            got["a3", q] = send(ta.at[q], ar3.at[q], s3.at[0, q], r3.at[0, q], at(OFFS[q], 0, 0, 0))

    stage2a(0)
    stage2b(0)
    stage2a(1)
    stage2b(1)
    stage3a(0)
    stage2c()
    stage2a(2)
    stage2b(2)
    stage3a(1)
    stage2a(3)
    stage2b(3)
    stage3a(2)
    for k in range(3):
        got["b2", k].wait_recv()
    tb[...] = sb[3] + br2[0] + br2[1] + br2[2]
    for k, o in enumerate(OFFS):
        got["b3", k] = send(tb.at[(x + o) % 4], br3.at[k], s3.at[1, k], r3.at[1, k], at(0, o, 0, 0))
    for k in range(3):
        got["c2", k].wait_recv()
    tc[...] = sc[pl.ds(x, 1)][0] + cr2[0] + cr2[1] + cr2[2]
    for k, o in enumerate(OFFS):
        got["c3", k] = send(tc.at[(y + o) % 4], cr3.at[k], s3.at[2, k], r3.at[2, k], at(0, 0, 0, o))
    stage3a(3)
    scale = 1.0 / math.sqrt(LENGTH * 4)
    for cp in bcopies:
        cp.wait_recv()
    bal = jnp.sum(bgat[...], axis=0) * (1.0 / LENGTH)
    bal_ref[0] = bal[0, 0]
    for k in range(3):
        got["a3", k].wait_recv()
    wg_ref[:RA, :128] = (ta[3] + ar3[0] + ar3[1] + ar3[2]) * scale
    for k in range(3):
        got["b3", k].wait_recv()
    wg_ref[:RA, 128:] = (tb[pl.ds(x, 1)][0] + br3[0] + br3[1] + br3[2]) * scale
    for k in range(3):
        got["c3", k].wait_recv()
    wg_ref[RA:, :] = (tc[pl.ds(y, 1)][0] + cr3[0] + cr3[1] + cr3[2]) * scale

    for cp in gcopies + bcopies + ccopies + sends:
        cp.wait_send()
    gout.wait()


def scratch():
    v = pltpu.VMEM
    s = pltpu.SemaphoreType.DMA
    n = len(PEERS)
    return [
        v((TOK, D), BF16), v((D, E), BF16), v((TOK, E), F32), v((TOK, E), F32), v((TOK, E), F32), v((TOK, E), BF16),
        v((8, 2, 2, 4 * ROWS, E), F32), v((8, 2, 4 * ROWS, E), F32),
        v((4, 4, 4, RA, 128), F32), v((4, 4, 4, RA, 128), F32), v((4, 4, 4, RC, E), F32),
        v((4, 3, 4, RA, 128), F32), v((4, 3, 4, RA, 128), F32), v((3, 4, 4, RC, E), F32),
        v((4, 4, RA, 128), F32), v((4, 4, RA, 128), F32), v((4, 4, RC, E), F32),
        v((4, 3, RA, 128), F32), v((3, 4, RA, 128), F32), v((3, 4, RC, E), F32),
        v((4, RA, 128), F32), v((4, RA, 128), F32), v((4, RC, E), F32),
        v((3, RA, 128), F32), v((3, RA, 128), F32), v((3, RC, E), F32),
        v((8, 128), F32), v((CTX, 8, 128), F32), v((8, 128), F32), v((CTX, 8, 128), F32), v((TOK, 2 * DOCS), BF16),
        s((NTCH,)), s, s, s((n,)), s((n,)), s((n,)), s((n,)), s((8,)), s((8,)),
        s((3, 4, 3)), s((3, 4, 3)), s((3, 4, 3)), s((3, 4, 3)), s((3, 3)), s((3, 3)),
    ]


def shards(hidden, router_weight, expert_ids, doc_lengths):
    vm = pl.BlockSpec(memory_space=pltpu.VMEM)
    hbm = pl.BlockSpec(memory_space=pl.ANY)
    balance, grad, weight_grad = pl.pallas_call(
        kernel,
        out_shape=(
            jax.ShapeDtypeStruct((1,), F32),
            jax.ShapeDtypeStruct((TOK, E), F32),
            jax.ShapeDtypeStruct((ROWS, E), F32),
        ),
        in_specs=[hbm, hbm, vm, vm],
        out_specs=(pl.BlockSpec(memory_space=pltpu.SMEM), hbm, vm),
        scratch_shapes=scratch(),
        compiler_params=pltpu.CompilerParams(
            collective_id=0, has_side_effects=True, vmem_limit_bytes=60 << 20
        ),
        name="balance_loss",
    )(hidden[0], router_weight, expert_ids[0].T, doc_lengths)
    return balance, grad[None], weight_grad


def solution(mesh):
    placed = (P("win", "ctx", None), P(), P("win", "ctx", None), P("win", None))
    return jax.shard_map(
        shards,
        mesh=mesh,
        in_specs=placed,
        out_specs=(P("win"), P("win", "ctx", None), P(("ctx", "win"), None)),
        check_vma=False,
    )
```

```python
import math

import jax
import jax.numpy as jnp
from jax import lax
from jax.experimental import pallas as pl
from jax.experimental.pallas import tpu as pltpu
from jax.sharding import PartitionSpec as P

MESH = pl.DeviceIdType.MESH
F32 = jnp.float32
BF16 = jnp.bfloat16

D, E, K = 7168, 256, 8
TOK = 1024
DOCS = 64
CTX = 32
LENGTH = TOK * CTX
TCH = 256
NTCH = TOK // TCH
GCH = 256
ROWS = D // 128
RA = 40
RC = ROWS - RA
CHUNK = 16 * ROWS
OFFS = (2, 1, 3)

NPEER = CTX - 1


def split2(v):
    hi = v.astype(BF16)
    lo = (v - hi.astype(F32)).astype(BF16)
    return hi, lo


def sigmoid(v):
    d = jnp.minimum(1.0 + jnp.exp(-v), 8e37)
    r = pl.reciprocal(d, approx=True)
    return r * (2.0 - d * r)


def dot(a, b):
    return jnp.dot(a, b, preferred_element_type=F32)


def loop(n, body, first=0):
    def step(i, carry):
        body(i)
        return carry

    lax.fori_loop(first, n, step, 0)


def kernel(
    hid, wgt, ids, lens_ref, bal_ref, grad_out, wg_ref,
    xs, ws, idt, picked, share, coef, gbf, loc, dw, crecv,
    pa, pb, pc, arl, brl, crl, ar1, br1, cr1, sa, sb, sc, ar2, br2, cr2, ta, tb, tc, ar3, br3, cr3,
    msg, gat, bmsg, bgat, member2,
    xsem, wsem, gss, grs, bss, brs, css, crs, s1, r1, sz, rz, s2, r2, s3, r3,
):
    ctx = lax.axis_index("ctx")
    y = lax.axis_index("win")
    z, x, c = ctx // 8, (ctx // 2) % 4, ctx % 2

    def at(dz=0, dx=0, dc=0, dy=0):
        return (((z + dz) % 4 * 4 + (x + dx) % 4) * 2 + (c + dc) % 2, (y + dy) % 4)

    def peer(k):
        n = 1 + (k + 19) % NPEER
        return at(n // 8, (n // 2) % 4, n % 2)

    def remote(src, dst, ssem, rsem, where):
        return pltpu.make_async_remote_copy(
            src_ref=src, dst_ref=dst, send_sem=ssem, recv_sem=rsem, device_id=where, device_id_type=MESH
        )

    wcopy = pltpu.make_async_copy(wgt, ws, wsem)
    wcopy.start(priority=0)

    def xcopy(t):
        rows = pl.ds(pl.multiple_of(t * TCH, TCH), TCH)
        return pltpu.make_async_copy(hid.at[rows], xs.at[rows], xsem.at[t])

    for t in range(NTCH):
        xcopy(t).start(priority=1)

    barrier = pltpu.get_barrier_semaphore()

    def greet(k):
        pl.semaphore_signal(barrier, inc=1, device_id=peer(k), device_id_type=MESH)

    loop(NPEER, greet)
    for dy in OFFS:
        pl.semaphore_signal(barrier, inc=1, device_id=at(dy=dy), device_id_type=MESH)

    lens = jnp.broadcast_to(lens_ref[...].astype(F32), (DOCS, DOCS))
    row = lax.broadcasted_iota(jnp.int32, (DOCS, DOCS), 0)
    col = lax.broadcasted_iota(jnp.int32, (DOCS, DOCS), 1)
    len_c = jnp.sum(jnp.where(row == col, lens, 0.0), axis=1, keepdims=True)
    end_c = jnp.sum(jnp.where(col <= row, lens, 0.0), axis=1, keepdims=True)
    start_c = end_c - len_c
    row2 = lax.broadcasted_iota(jnp.int32, (DOCS, 2 * DOCS), 0)
    col2 = lax.broadcasted_iota(jnp.int32, (DOCS, 2 * DOCS), 1) % DOCS
    end_r = jnp.sum(jnp.where(row2 <= col2, len_c, 0.0), axis=0, keepdims=True)
    start_r = jnp.sum(jnp.where(row2 < col2, len_c, 0.0), axis=0, keepdims=True)
    base = (ctx * TOK).astype(F32)

    def inside(lo, hi, pos):
        return (lo <= pos) & (pos < hi)

    sel_first = inside(start_c, end_c, base)
    sel_last = inside(start_c, end_c, base + (TOK - 1))

    idt[...] = ids[...].astype(F32).T
    lane = lax.broadcasted_iota(jnp.int32, (TCH, E), 1).astype(F32)

    def choose(t):
        rows = pl.ds(pl.multiple_of(t * TCH, TCH), TCH)
        own = idt[rows, :]
        hit = own[:, 0:1] == lane
        for k in range(1, K):
            hit = hit | (own[:, k : k + 1] == lane)
        picked[rows, :] = jnp.where(hit, 1.0, 0.0)
        pos = lax.broadcasted_iota(jnp.int32, (TCH, 2 * DOCS), 0).astype(F32) + (base + (t * TCH).astype(F32))
        member2[rows, :] = jnp.where(inside(start_r, end_r, pos), 1.0, 0.0).astype(BF16)

    loop(NTCH, choose)

    loc[...] = jnp.zeros_like(loc)

    def forward(t, logits):
        rows = pl.ds(pl.multiple_of(jnp.maximum(t, 0) * TCH, TCH), TCH)
        aff = sigmoid(logits)
        total = jnp.sum(aff, axis=-1, keepdims=True)
        sh = aff * (1.0 / total)
        share[rows, :] = sh
        coef[rows, :] = (float(E) * sh) * (1.0 - aff)
        chosen = picked[rows, :] * aff
        gate = chosen * (1.0 / jnp.sum(chosen, axis=-1, keepdims=True))
        origin = jnp.where(t < 0, -4.0 * LENGTH, base + (t * TCH).astype(F32))
        pos = lax.broadcasted_iota(jnp.int32, (DOCS, TCH), 1).astype(F32) + origin
        mem = jnp.where(inside(start_c, end_c, pos), 1.0, 0.0).astype(BF16)
        loc[...] += dot(mem, jnp.concatenate(split2(gate), axis=1))

    wcopy.wait()

    def ahead(t, logits):
        xcopy(t).wait()
        rows = pl.ds(pl.multiple_of(t * TCH, TCH), TCH)
        new = dot(xs[rows, :], ws[...])
        forward(t - 1, logits)
        return new

    logits = lax.fori_loop(0, NTCH, ahead, jnp.zeros((TCH, E), F32))
    forward(jnp.int32(NTCH - 1), logits)
    local = loc[:, :E] + loc[:, E:]

    first = jnp.sum(jnp.where(sel_first, local, 0.0), axis=0, keepdims=True)
    last = jnp.sum(jnp.where(sel_last, local, 0.0), axis=0, keepdims=True)
    tile = jnp.concatenate(
        [first[:, :128], first[:, 128:], last[:, :128], last[:, 128:], jnp.zeros((4, 128), F32)], axis=0
    )
    msg[...] = tile
    gat[pl.ds(ctx, 1)] = tile[None]

    pl.semaphore_wait(barrier, NPEER + len(OFFS))

    def spread(src, dst, ssem, rsem):
        loop(NPEER, lambda k: remote(src, dst.at[ctx], ssem, rsem, peer(k)).start())

    def everyones(dst, ssem, rsem):
        part = dst.at[pl.ds(0, NPEER)]
        return remote(part, part, ssem, rsem, at(dc=1))

    spread(msg, gat, gss, grs)

    gcol = lax.broadcasted_iota(jnp.int32, (2 * DOCS, 8 * CTX), 1)
    grow = lax.broadcasted_iota(jnp.int32, (2 * DOCS, 8 * CTX), 0)
    kind = gcol % 8
    gpos = ((gcol // 8) * TOK).astype(F32)
    start2 = jnp.concatenate([start_c, start_c], axis=0)
    end2 = jnp.concatenate([end_c, end_c], axis=0)
    half = grow // DOCS
    s_first = (kind == half) & inside(start2, end2, gpos)
    s_last = (kind == half + 2) & inside(start2, end2, gpos + (TOK - 1)) & (start2 > gpos)
    smat = jnp.where(s_first | s_last, 1.0, 0.0).astype(BF16)

    everyones(gat, gss, grs).wait_recv()
    ghi, glo = split2(gat[...].reshape(8 * CTX, 128))
    sums = dot(smat, jnp.concatenate([ghi, glo], axis=1))
    sums = sums[:, :128] + sums[:, 128:]
    counts = jnp.concatenate([sums[:DOCS], sums[DOCS:]], axis=1)
    counts = counts + jnp.where(sel_first | sel_last, 0.0, local)
    rates = counts * float(E) / len_c
    rates2 = jnp.concatenate(split2(rates), axis=0)

    def backward(t, gsum):
        rows = pl.ds(pl.multiple_of(t * GCH, GCH), GCH)
        tr = dot(member2[rows, :], rates2)
        mean = jnp.sum(tr * share[rows, :], axis=-1, keepdims=True)
        g = coef[rows, :] * (tr - mean)
        grad_out[rows, :] = g
        gbf[rows, :] = g.astype(BF16)
        return gsum + jnp.sum(mean, axis=0, keepdims=True)

    gsum = lax.fori_loop(0, TOK // GCH, backward, jnp.zeros((1, 1), F32))
    btile = jnp.broadcast_to(gsum, (8, 128))
    bmsg[...] = btile
    bgat[pl.ds(ctx, 1)] = btile[None]

    def ahead_z(q):
        return (2 + 3 * q + 3 * (q // 2) + 2 * (q // 3)) % 4

    def core_copy(i):
        return remote(dw.at[i, :, 1 - c], crecv.at[i], css.at[i], crs.at[i], at(dc=1))

    def second(i):
        zq = (z + ahead_z(i // 2)) % 4
        off = pl.multiple_of(zq * (2 * CHUNK) + (i % 2) * CHUNK, 128)
        prod = lax.dot_general(
            xs[:, pl.ds(off, CHUNK)], gbf[...], (((0,), (0,)), ((), ())), preferred_element_type=F32
        )
        dw[i] = prod.reshape(2, 2, 4 * ROWS, E)
        core_copy(i).start()

    def core_sum(i):
        core_copy(i).wait_recv()
        q = i // 2
        for xi in range(2):
            xd = 2 * (i % 2) + xi
            v = (dw[i, xi, pl.ds(c, 1)][0] + crecv[i, xi]).reshape(4, ROWS, E)
            pa[q, xd] = v[:, :RA, :128]
            for yd in range(4):
                pb[q, yd, xd] = v[yd, :RA, 128:]
            pc[q, xd] = v[:, RA:, :]

    H0, H1 = pl.ds(0, 2), pl.ds(2, 2)

    def ring(part, q, kind):
        p, rl, r, me = (pa, arl, ar1, x) if part == 0 else (pb, brl, br1, y)
        step = 1 if kind % 2 == 0 else 3
        where = at(dx=step) if part == 0 else at(dy=step)
        opposite, side = (me + 2) % 4, (me + step) % 4
        src, dst = (
            (p.at[q, opposite, H0], rl.at[q, 0]),
            (p.at[q, opposite, H1], rl.at[q, 1]),
            (p.at[q, side, H1], r.at[q, 0, H1]),
            (p.at[q, side, H0], r.at[q, 1, H0]),
            (p.at[q, side, H0], r.at[q, 0, H0]),
            (p.at[q, side, H1], r.at[q, 1, H1]),
        )[kind]
        return remote(src, dst, s1.at[part, q, kind], r1.at[part, q, kind], where)

    def ring_z(kind):
        src, dst = (
            (pc.at[0, H0], crl.at[0]),
            (pc.at[0, H1], crl.at[1]),
            (pc.at[1, H1], cr1.at[0, H1]),
            (pc.at[2, H0], cr1.at[1, H0]),
            (pc.at[1, H0], cr1.at[0, H0]),
            (pc.at[2, H1], cr1.at[1, H1]),
        )[kind]
        return remote(src, dst, sz.at[kind], rz.at[kind], at(dz=1 if kind % 2 == 0 else 3))

    def p1(q):
        for kind in range(4):
            ring(0, q, kind).start()
            ring(1, q, kind).start()

        @pl.when(q == 0)
        def _():
            ring_z(0).start()
            ring_z(1).start()

        @pl.when(q == 1)
        def _():
            ring_z(2).start()

        @pl.when(q == 2)
        def _():
            ring_z(3).start()

    def p2(q):
        for part in range(2):
            p, rl, me = ((pa, arl, x), (pb, brl, y))[part]
            for d, (step, h) in enumerate(((1, H0), (3, H1))):
                ring(part, q, d).wait_recv()
                side = (me + step) % 4
                p[q, pl.ds(side, 1), h] = p[q, pl.ds(side, 1), h] + rl[q, pl.ds(d, 1)]
                ring(part, q, 4 + d).start()

        @pl.when(q == 1)
        def _():
            ring_z(0).wait_recv()
            pc[1, H0] = pc[1, H0] + crl[0]
            ring_z(4).start()

        @pl.when(q == 2)
        def _():
            ring_z(1).wait_recv()
            pc[2, H1] = pc[2, H1] + crl[1]
            ring_z(5).start()

    def a2(q, k):
        return remote(sa.at[q, (y + OFFS[k]) % 4], ar2.at[q, k], s2.at[0, q, k], r2.at[0, q, k], at(dy=OFFS[k]))

    def b2(q):
        return remote(sb.at[q], br2.at[q], s2.at[1, q, 0], r2.at[1, q, 0], at(dz=ahead_z(q)))

    def c2(k):
        return remote(sc.at[(x + OFFS[k]) % 4], cr2.at[k], s2.at[1, 3, k], r2.at[1, 3, k], at(dx=OFFS[k]))

    def a3(q):
        return remote(ta.at[q], ar3.at[q], s3.at[0, q], r3.at[0, q], at(dz=ahead_z(q)))

    def b3(k):
        return remote(tb.at[(x + OFFS[k]) % 4], br3.at[k], s3.at[1, k], r3.at[1, k], at(dx=OFFS[k]))

    def c3(k):
        return remote(tc.at[(y + OFFS[k]) % 4], cr3.at[k], s3.at[2, k], r3.at[2, k], at(dy=OFFS[k]))

    def p3(q):
        for kind in range(2, 6):
            ring(0, q, kind).wait_recv()
        sa[q] = pa[q, pl.ds(x, 1)][0] + ar1[q, 0] + ar1[q, 1]
        for k in range(3):
            a2(q, k).start()
        for kind in range(2, 6):
            ring(1, q, kind).wait_recv()
        sb[q] = pb[q, pl.ds(y, 1)][0] + br1[q, 0] + br1[q, 1]

        @pl.when(q < 3)
        def _():
            b2(q).start()

        for kind in range(4):
            ring(0, q, kind).wait_send()
            ring(1, q, kind).wait_send()

    def p4(q):
        for k in range(3):
            a2(q, k).wait_recv()
        ta[q] = sa[q, pl.ds(y, 1)][0] + ar2[q, 0] + ar2[q, 1] + ar2[q, 2]

        @pl.when(q < 3)
        def _():
            a3(q).start()

        for kind in range(4, 6):
            ring(0, q, kind).wait_send()
            ring(1, q, kind).wait_send()

    def slot(j):
        @pl.when(j < 4)
        def _():
            loop(2 * j + 2, second, 2 * j)

        @pl.when((j >= 2) & (j < 6))
        def _():
            p3(j - 2)

        @pl.when((j >= 1) & (j < 5))
        def _():
            p2(j - 1)

        @pl.when(j < 4)
        def _():
            loop(2 * j + 2, core_sum, 2 * j)
            p1(j)

        @pl.when(j == 0)
        def _():
            spread(bmsg, bgat, bss, brs)

        @pl.when(j == 4)
        def _():
            for kind in range(2, 6):
                ring_z(kind).wait_recv()
            sc[...] = pc[3] + cr1[0] + cr1[1]
            for k in range(3):
                c2(k).start()

        @pl.when(j == 5)
        def _():
            for q in range(3):
                b2(q).wait_recv()
            tb[...] = sb[3] + br2[0] + br2[1] + br2[2]
            for k in range(3):
                b3(k).start()
            for k in range(3):
                c2(k).wait_recv()
            tc[...] = sc[pl.ds(x, 1)][0] + cr2[0] + cr2[1] + cr2[2]
            for k in range(3):
                c3(k).start()

        @pl.when(j >= 3)
        def _():
            p4(j - 3)

    loop(7, slot)

    everyones(bgat, bss, brs).wait_recv()
    bal = jnp.sum(bgat[...], axis=0) * (1.0 / LENGTH)
    bal_ref[0] = bal[0, 0]
    loop(8, lambda i: core_copy(i).wait_send())
    everyones(gat, gss, grs).wait_send()
    everyones(bgat, bss, brs).wait_send()
    for kind in range(6):
        ring_z(kind).wait_send()
    for k in range(3):
        for q in range(4):
            a2(q, k).wait_send()
        b2(k).wait_send()
        c2(k).wait_send()
    scale = 1.0 / math.sqrt(LENGTH * 4)
    for k in range(3):
        a3(k).wait_recv()
    wg_ref[:RA, :128] = (ta[3] + ar3[0] + ar3[1] + ar3[2]) * scale
    for k in range(3):
        b3(k).wait_recv()
    wg_ref[:RA, 128:] = (tb[pl.ds(x, 1)][0] + br3[0] + br3[1] + br3[2]) * scale
    for k in range(3):
        c3(k).wait_recv()
    wg_ref[RA:, :] = (tc[pl.ds(y, 1)][0] + cr3[0] + cr3[1] + cr3[2]) * scale
    for k in range(3):
        a3(k).wait_send()
        b3(k).wait_send()
        c3(k).wait_send()


def scratch():
    v = pltpu.VMEM
    s = pltpu.SemaphoreType.DMA
    return [
        v((TOK, D), BF16), v((D, E), BF16), v((TOK, K), F32), v((TOK, E), F32), v((TOK, E), F32), v((TOK, E), F32),
        v((TOK, E), BF16), v((DOCS, 2 * E), F32),
        v((8, 2, 2, 4 * ROWS, E), F32), v((8, 2, 4 * ROWS, E), F32),
        v((4, 4, 4, RA, 128), F32), v((4, 4, 4, RA, 128), F32), v((4, 4, 4, RC, E), F32),
        v((4, 2, 2, RA, 128), F32), v((4, 2, 2, RA, 128), F32), v((2, 2, 4, RC, E), F32),
        v((4, 2, 4, RA, 128), F32), v((4, 2, 4, RA, 128), F32), v((2, 4, 4, RC, E), F32),
        v((4, 4, RA, 128), F32), v((4, 4, RA, 128), F32), v((4, 4, RC, E), F32),
        v((4, 3, RA, 128), F32), v((3, 4, RA, 128), F32), v((3, 4, RC, E), F32),
        v((4, RA, 128), F32), v((4, RA, 128), F32), v((4, RC, E), F32),
        v((3, RA, 128), F32), v((3, RA, 128), F32), v((3, RC, E), F32),
        v((8, 128), F32), v((CTX, 8, 128), F32), v((8, 128), F32), v((CTX, 8, 128), F32), v((TOK, 2 * DOCS), BF16),
        s((NTCH,)), s, s, s, s, s, s((8,)), s((8,)),
        s((2, 4, 6)), s((2, 4, 6)), s((6,)), s((6,)), s((2, 4, 3)), s((2, 4, 3)), s((3, 3)), s((3, 3)),
    ]


def shards(hidden, router_weight, expert_ids, doc_lengths):
    vm = pl.BlockSpec(memory_space=pltpu.VMEM)
    hbm = pl.BlockSpec(memory_space=pl.ANY)
    balance, grad, weight_grad = pl.pallas_call(
        kernel,
        out_shape=(
            jax.ShapeDtypeStruct((1,), F32),
            pltpu.VMEM((TOK, E), F32),
            pltpu.VMEM((ROWS, E), F32),
        ),
        in_specs=[hbm, hbm, vm, vm],
        out_specs=(pl.BlockSpec(memory_space=pltpu.SMEM), vm, vm),
        scratch_shapes=scratch(),
        compiler_params=pltpu.CompilerParams(
            collective_id=0, has_side_effects=True, vmem_limit_bytes=60 << 20
        ),
        name="balance_loss",
    )(hidden[0], router_weight, expert_ids[0].T, doc_lengths)
    return balance, grad[None], weight_grad


def solution(mesh):
    placed = (P("win", "ctx", None), P(), P("win", "ctx", None), P("win", None))
    return jax.shard_map(
        shards,
        mesh=mesh,
        in_specs=placed,
        out_specs=(P("win"), P("win", "ctx", None), P(("ctx", "win"), None)),
        check_vma=False,
    )
```

```python
import math

import jax
import jax.numpy as jnp
from jax import lax
from jax.experimental import pallas as pl
from jax.experimental.pallas import tpu as pltpu
from jax.sharding import PartitionSpec as P

MESH = pl.DeviceIdType.MESH
F32 = jnp.float32
BF16 = jnp.bfloat16

D, E, K = 7168, 256, 8
TOK = 1024
DOCS = 64
CTX = 32
LENGTH = TOK * CTX
TCH = 256
NTCH = TOK // TCH
GCH = 256
ROWS = D // 128
RA = 40
RC = ROWS - RA
CHUNK = 16 * ROWS
OFFS = (2, 1, 3)

NPEER = CTX - 1


def split2(v):
    hi = v.astype(BF16)
    lo = (v - hi.astype(F32)).astype(BF16)
    return hi, lo


def sigmoid(v):
    d = jnp.minimum(1.0 + jnp.exp(-v), 8e37)
    r = pl.reciprocal(d, approx=True)
    return r * (2.0 - d * r)


def dot(a, b):
    return jnp.dot(a, b, preferred_element_type=F32)


def loop(n, body, first=0):
    def step(i, carry):
        body(i)
        return carry

    lax.fori_loop(first, n, step, 0)


def kernel(
    hid, wgt, ids_in, lens_in, bal_ref, grad_out, wg_ref,
    ids, lens_ref, xs, ws, idt, picked, share, coef, gbf, loc, dw, crecv,
    pa, pb, pc, arl, brl, crl, ar1, br1, cr1, sa, sb, sc, ar2, br2, cr2, ta, tb, tc, ar3, br3, cr3,
    msg, gat, bmsg, bgat, member2,
    isem, xsem, wsem, gss, grs, bss, brs, css, crs, s1, r1, sz, rz, s2, r2, s3, r3,
):
    ctx = lax.axis_index("ctx")
    y = lax.axis_index("win")
    z, x, c = ctx // 8, (ctx // 2) % 4, ctx % 2

    def at(dz=0, dx=0, dc=0, dy=0):
        return (((z + dz) % 4 * 4 + (x + dx) % 4) * 2 + (c + dc) % 2, (y + dy) % 4)

    def peer(k):
        n = 1 + (k + 19) % NPEER
        return at(n // 8, (n // 2) % 4, n % 2)

    def remote(src, dst, ssem, rsem, where):
        return pltpu.make_async_remote_copy(
            src_ref=src, dst_ref=dst, send_sem=ssem, recv_sem=rsem, device_id=where, device_id_type=MESH
        )

    small = [pltpu.make_async_copy(a, b, isem.at[k]) for k, (a, b) in enumerate(((lens_in, lens_ref), (ids_in, ids)))]
    for cp in small:
        cp.start(priority=0)
    wcopy = pltpu.make_async_copy(wgt, ws, wsem)
    wcopy.start(priority=0)

    def xcopy(t):
        rows = pl.ds(pl.multiple_of(t * TCH, TCH), TCH)
        return pltpu.make_async_copy(hid.at[rows], xs.at[rows], xsem.at[t])

    for t in range(NTCH):
        xcopy(t).start(priority=1)

    barrier = pltpu.get_barrier_semaphore()

    def greet(k):
        pl.semaphore_signal(barrier, inc=1, device_id=peer(k), device_id_type=MESH)

    loop(NPEER, greet)
    for dy in OFFS:
        pl.semaphore_signal(barrier, inc=1, device_id=at(dy=dy), device_id_type=MESH)

    for cp in small:
        cp.wait()

    lens = jnp.broadcast_to(lens_ref[...].astype(F32), (DOCS, DOCS))
    row = lax.broadcasted_iota(jnp.int32, (DOCS, DOCS), 0)
    col = lax.broadcasted_iota(jnp.int32, (DOCS, DOCS), 1)
    len_c = jnp.sum(jnp.where(row == col, lens, 0.0), axis=1, keepdims=True)
    end_c = jnp.sum(jnp.where(col <= row, lens, 0.0), axis=1, keepdims=True)
    start_c = end_c - len_c
    row2 = lax.broadcasted_iota(jnp.int32, (DOCS, 2 * DOCS), 0)
    col2 = lax.broadcasted_iota(jnp.int32, (DOCS, 2 * DOCS), 1) % DOCS
    end_r = jnp.sum(jnp.where(row2 <= col2, len_c, 0.0), axis=0, keepdims=True)
    start_r = jnp.sum(jnp.where(row2 < col2, len_c, 0.0), axis=0, keepdims=True)
    base = (ctx * TOK).astype(F32)

    def inside(lo, hi, pos):
        return (lo <= pos) & (pos < hi)

    sel_first = inside(start_c, end_c, base)
    sel_last = inside(start_c, end_c, base + (TOK - 1))

    idt[...] = ids[...].astype(F32).T
    lane = lax.broadcasted_iota(jnp.int32, (TCH, E), 1).astype(F32)

    def choose(t):
        rows = pl.ds(pl.multiple_of(t * TCH, TCH), TCH)
        own = idt[rows, :]
        hit = own[:, 0:1] == lane
        for k in range(1, K):
            hit = hit | (own[:, k : k + 1] == lane)
        picked[rows, :] = jnp.where(hit, 1.0, 0.0)
        pos = lax.broadcasted_iota(jnp.int32, (TCH, 2 * DOCS), 0).astype(F32) + (base + (t * TCH).astype(F32))
        member2[rows, :] = jnp.where(inside(start_r, end_r, pos), 1.0, 0.0).astype(BF16)

    loop(NTCH, choose)

    loc[...] = jnp.zeros_like(loc)

    def forward(t, logits):
        rows = pl.ds(pl.multiple_of(jnp.maximum(t, 0) * TCH, TCH), TCH)
        aff = sigmoid(logits)
        total = jnp.sum(aff, axis=-1, keepdims=True)
        sh = aff * (1.0 / total)
        share[rows, :] = sh
        coef[rows, :] = (float(E) * sh) * (1.0 - aff)
        chosen = picked[rows, :] * aff
        gate = chosen * (1.0 / jnp.sum(chosen, axis=-1, keepdims=True))
        origin = jnp.where(t < 0, -4.0 * LENGTH, base + (t * TCH).astype(F32))
        pos = lax.broadcasted_iota(jnp.int32, (DOCS, TCH), 1).astype(F32) + origin
        mem = jnp.where(inside(start_c, end_c, pos), 1.0, 0.0).astype(BF16)
        loc[...] += dot(mem, jnp.concatenate(split2(gate), axis=1))

    wcopy.wait()

    def ahead(t, logits):
        xcopy(t).wait()
        rows = pl.ds(pl.multiple_of(t * TCH, TCH), TCH)
        new = dot(xs[rows, :], ws[...])
        forward(t - 1, logits)
        return new

    logits = lax.fori_loop(0, NTCH, ahead, jnp.zeros((TCH, E), F32))
    forward(jnp.int32(NTCH - 1), logits)
    local = loc[:, :E] + loc[:, E:]

    first = jnp.sum(jnp.where(sel_first, local, 0.0), axis=0, keepdims=True)
    last = jnp.sum(jnp.where(sel_last, local, 0.0), axis=0, keepdims=True)
    tile = jnp.concatenate(
        [first[:, :128], first[:, 128:], last[:, :128], last[:, 128:], jnp.zeros((4, 128), F32)], axis=0
    )
    msg[...] = tile
    gat[pl.ds(ctx, 1)] = tile[None]

    pl.semaphore_wait(barrier, NPEER + len(OFFS))

    def spread(src, dst, ssem, rsem):
        loop(NPEER, lambda k: remote(src, dst.at[ctx], ssem, rsem, peer(k)).start())

    def everyones(dst, ssem, rsem):
        part = dst.at[pl.ds(0, NPEER)]
        return remote(part, part, ssem, rsem, at(dc=1))

    spread(msg, gat, gss, grs)

    gcol = lax.broadcasted_iota(jnp.int32, (2 * DOCS, 8 * CTX), 1)
    grow = lax.broadcasted_iota(jnp.int32, (2 * DOCS, 8 * CTX), 0)
    kind = gcol % 8
    gpos = ((gcol // 8) * TOK).astype(F32)
    start2 = jnp.concatenate([start_c, start_c], axis=0)
    end2 = jnp.concatenate([end_c, end_c], axis=0)
    half = grow // DOCS
    s_first = (kind == half) & inside(start2, end2, gpos)
    s_last = (kind == half + 2) & inside(start2, end2, gpos + (TOK - 1)) & (start2 > gpos)
    smat = jnp.where(s_first | s_last, 1.0, 0.0).astype(BF16)

    everyones(gat, gss, grs).wait_recv()
    ghi, glo = split2(gat[...].reshape(8 * CTX, 128))
    sums = dot(smat, jnp.concatenate([ghi, glo], axis=1))
    sums = sums[:, :128] + sums[:, 128:]
    counts = jnp.concatenate([sums[:DOCS], sums[DOCS:]], axis=1)
    counts = counts + jnp.where(sel_first | sel_last, 0.0, local)
    rates = counts * float(E) / len_c
    rates2 = jnp.concatenate(split2(rates), axis=0)

    def backward(t, gsum):
        rows = pl.ds(pl.multiple_of(t * GCH, GCH), GCH)
        tr = dot(member2[rows, :], rates2)
        mean = jnp.sum(tr * share[rows, :], axis=-1, keepdims=True)
        g = coef[rows, :] * (tr - mean)
        grad_out[rows, :] = g
        gbf[rows, :] = g.astype(BF16)
        return gsum + jnp.sum(mean, axis=0, keepdims=True)

    gsum = lax.fori_loop(0, TOK // GCH, backward, jnp.zeros((1, 1), F32))
    btile = jnp.broadcast_to(gsum, (1, 128))
    bmsg[...] = btile
    bgat[pl.ds(ctx, 1)] = btile[None]

    def ahead_z(q):
        return (2 + 3 * q + 3 * (q // 2) + 2 * (q // 3)) % 4

    other = 1 - x // 2

    def core_copy(i):
        return remote(dw.at[i, :, 1 - c], crecv.at[i], css.at[i], crs.at[i], at(dc=1))

    def second(i):
        zq = (z + ahead_z(i // 2)) % 4
        off = pl.multiple_of(zq * (2 * CHUNK) + (other + i) % 2 * CHUNK, 128)
        prod = lax.dot_general(
            xs[:, pl.ds(off, CHUNK)], gbf[...], (((0,), (0,)), ((), ())), preferred_element_type=F32
        )
        dw[i] = prod.reshape(2, 2, 4 * ROWS, E)
        core_copy(i).start()

    def core_sum(i):
        core_copy(i).wait_recv()
        q = i // 2
        for xi in range(2):
            xd = 2 * ((other + i) % 2) + xi
            v = (dw[i, xi, pl.ds(c, 1)][0] + crecv[i, xi]).reshape(4, ROWS, E)
            pa[q, xd] = v[:, :RA, :128]
            for yd in range(4):
                pb[q, yd, xd] = v[yd, :RA, 128:]
            pc[q, xd] = v[:, RA:, :]

    H0, H1 = pl.ds(0, 2), pl.ds(2, 2)

    def ring(part, q, kind):
        p, rl, r, me = (pa, arl, ar1, x) if part == 0 else (pb, brl, br1, y)
        step = 1 if kind % 2 == 0 else 3
        where = at(dx=step) if part == 0 else at(dy=step)
        opposite, side = (me + 2) % 4, (me + step) % 4
        src, dst = (
            (p.at[q, opposite, H0], rl.at[q, 0]),
            (p.at[q, opposite, H1], rl.at[q, 1]),
            (p.at[q, side, H1], r.at[q, 0, H1]),
            (p.at[q, side, H0], r.at[q, 1, H0]),
            (p.at[q, side, H0], r.at[q, 0, H0]),
            (p.at[q, side, H1], r.at[q, 1, H1]),
        )[kind]
        return remote(src, dst, s1.at[part, q, kind], r1.at[part, q, kind], where)

    def ring_z(kind):
        src, dst = (
            (pc.at[0, H0], crl.at[0]),
            (pc.at[0, H1], crl.at[1]),
            (pc.at[1, H1], cr1.at[0, H1]),
            (pc.at[2, H0], cr1.at[1, H0]),
            (pc.at[1, H0], cr1.at[0, H0]),
            (pc.at[2, H1], cr1.at[1, H1]),
        )[kind]
        return remote(src, dst, sz.at[kind], rz.at[kind], at(dz=1 if kind % 2 == 0 else 3))

    def p1(i):
        q = i // 2
        half = (other + i) % 2

        @pl.when(half == 0)
        def _():
            @pl.when(q == 0)
            def _():
                ring_z(0).start()

            @pl.when(q == 2)
            def _():
                ring_z(3).start()

            ring(1, q, 0).start()
            ring(1, q, 3).start()

        @pl.when(half == 1)
        def _():
            @pl.when(q == 0)
            def _():
                ring_z(1).start()

            @pl.when(q == 1)
            def _():
                ring_z(2).start()

            ring(1, q, 1).start()
            ring(1, q, 2).start()

        @pl.when(i % 2 == 0)
        def _():
            ring(0, q, 0).start()
            ring(0, q, 1).start()

        @pl.when((x + i) % 2 == 0)
        def _():
            ring(0, q, 3).start()

        @pl.when((x + i) % 2 == 1)
        def _():
            ring(0, q, 2).start()

    def p2(q):
        for part in range(2):
            p, rl, me = ((pa, arl, x), (pb, brl, y))[part]
            for d, (step, h) in enumerate(((1, H0), (3, H1))):
                ring(part, q, d).wait_recv()
                side = (me + step) % 4
                p[q, pl.ds(side, 1), h] = p[q, pl.ds(side, 1), h] + rl[q, pl.ds(d, 1)]
                ring(part, q, 4 + d).start()

    def p2_z():
        ring_z(0).wait_recv()
        pc[1, H0] = pc[1, H0] + crl[0]
        ring_z(4).start()
        ring_z(1).wait_recv()
        pc[2, H1] = pc[2, H1] + crl[1]
        ring_z(5).start()

    def a2(q, k):
        return remote(sa.at[q, (y + OFFS[k]) % 4], ar2.at[q, k], s2.at[0, q, k], r2.at[0, q, k], at(dy=OFFS[k]))

    def b2(q):
        return remote(sb.at[q], br2.at[q], s2.at[1, q, 0], r2.at[1, q, 0], at(dz=ahead_z(q)))

    def c2(k):
        return remote(sc.at[(x + OFFS[k]) % 4], cr2.at[k], s2.at[1, 3, k], r2.at[1, 3, k], at(dx=OFFS[k]))

    def a3(q):
        return remote(ta.at[q], ar3.at[q], s3.at[0, q], r3.at[0, q], at(dz=ahead_z(q)))

    def b3(k):
        return remote(tb.at[(x + OFFS[k]) % 4], br3.at[k], s3.at[1, k], r3.at[1, k], at(dx=OFFS[k]))

    def c3(k):
        return remote(tc.at[(y + OFFS[k]) % 4], cr3.at[k], s3.at[2, k], r3.at[2, k], at(dy=OFFS[k]))

    def p3(q):
        for kind in range(2, 6):
            ring(0, q, kind).wait_recv()
        sa[q] = pa[q, pl.ds(x, 1)][0] + ar1[q, 0] + ar1[q, 1]
        for k in range(3):
            a2(q, k).start()
        for kind in range(2, 6):
            ring(1, q, kind).wait_recv()
        sb[q] = pb[q, pl.ds(y, 1)][0] + br1[q, 0] + br1[q, 1]

        @pl.when(q < 3)
        def _():
            b2(q).start()

        for kind in range(4):
            ring(0, q, kind).wait_send()
            ring(1, q, kind).wait_send()

    def p4(q):
        for k in range(3):
            a2(q, k).wait_recv()
        ta[q] = sa[q, pl.ds(y, 1)][0] + ar2[q, 0] + ar2[q, 1] + ar2[q, 2]

        @pl.when(q < 3)
        def _():
            a3(q).start()

        for kind in range(4, 6):
            ring(0, q, kind).wait_send()
            ring(1, q, kind).wait_send()

    def slot(i):
        @pl.when(i < 8)
        def _():
            second(i)

        @pl.when((i >= 2) & (i < 10))
        def _():
            core_sum(i - 2)
            p1(i - 2)

        @pl.when(i == 10)
        def _():
            spread(bmsg, bgat, bss, brs)

        @pl.when((i >= 9) & (i < 11))
        def _():
            p3(i - 9)

        @pl.when((i >= 5) & (i < 12) & (i % 2 == 1))
        def _():
            p2((i - 5) // 2)

        @pl.when(i == 7)
        def _():
            p2_z()

        @pl.when(i == 11)
        def _():
            for kind in range(2, 6):
                ring_z(kind).wait_recv()
            sc[...] = pc[3] + cr1[0] + cr1[1]
            for k in range(3):
                c2(k).start()

        @pl.when((i >= 11) & (i < 13))
        def _():
            p3(i - 9)

        @pl.when(i >= 11)
        def _():
            p4(i - 11)

        @pl.when(i == 13)
        def _():
            for q in range(3):
                b2(q).wait_recv()
            tb[...] = sb[3] + br2[0] + br2[1] + br2[2]
            for k in range(3):
                b3(k).start()
            for k in range(3):
                c2(k).wait_recv()
            tc[...] = sc[pl.ds(x, 1)][0] + cr2[0] + cr2[1] + cr2[2]
            for k in range(3):
                c3(k).start()

    loop(15, slot)

    everyones(bgat, bss, brs).wait_recv()
    bal = jnp.sum(bgat[...], axis=0) * (1.0 / LENGTH)
    bal_ref[0] = bal[0, 0]
    loop(8, lambda i: core_copy(i).wait_send())
    everyones(gat, gss, grs).wait_send()
    everyones(bgat, bss, brs).wait_send()
    for kind in range(6):
        ring_z(kind).wait_send()
    for k in range(3):
        for q in range(4):
            a2(q, k).wait_send()
        b2(k).wait_send()
        c2(k).wait_send()
    scale = 1.0 / math.sqrt(LENGTH * 4)
    for k in range(3):
        a3(k).wait_recv()
    wg_ref[:RA, :128] = (ta[3] + ar3[0] + ar3[1] + ar3[2]) * scale
    for k in range(3):
        b3(k).wait_recv()
    wg_ref[:RA, 128:] = (tb[pl.ds(x, 1)][0] + br3[0] + br3[1] + br3[2]) * scale
    for k in range(3):
        c3(k).wait_recv()
    wg_ref[RA:, :] = (tc[pl.ds(y, 1)][0] + cr3[0] + cr3[1] + cr3[2]) * scale
    for k in range(3):
        a3(k).wait_send()
        b3(k).wait_send()
        c3(k).wait_send()


def scratch():
    v = pltpu.VMEM
    s = pltpu.SemaphoreType.DMA
    return [
        v((K, TOK), jnp.int32), v((1, DOCS), jnp.int32),
        v((TOK, D), BF16), v((D, E), BF16), v((TOK, K), F32), v((TOK, E), F32), v((TOK, E), F32), v((TOK, E), F32),
        v((TOK, E), BF16), v((DOCS, 2 * E), F32),
        v((8, 2, 2, 4 * ROWS, E), F32), v((8, 2, 4 * ROWS, E), F32),
        v((4, 4, 4, RA, 128), F32), v((4, 4, 4, RA, 128), F32), v((4, 4, 4, RC, E), F32),
        v((4, 2, 2, RA, 128), F32), v((4, 2, 2, RA, 128), F32), v((2, 2, 4, RC, E), F32),
        v((4, 2, 4, RA, 128), F32), v((4, 2, 4, RA, 128), F32), v((2, 4, 4, RC, E), F32),
        v((4, 4, RA, 128), F32), v((4, 4, RA, 128), F32), v((4, 4, RC, E), F32),
        v((4, 3, RA, 128), F32), v((3, 4, RA, 128), F32), v((3, 4, RC, E), F32),
        v((4, RA, 128), F32), v((4, RA, 128), F32), v((4, RC, E), F32),
        v((3, RA, 128), F32), v((3, RA, 128), F32), v((3, RC, E), F32),
        v((8, 128), F32), v((CTX, 8, 128), F32), v((1, 128), F32), v((CTX, 1, 128), F32), v((TOK, 2 * DOCS), BF16),
        s((2,)), s((NTCH,)), s, s, s, s, s, s((8,)), s((8,)),
        s((2, 4, 6)), s((2, 4, 6)), s((6,)), s((6,)), s((2, 4, 3)), s((2, 4, 3)), s((3, 3)), s((3, 3)),
    ]


def shards(hidden, router_weight, expert_ids, doc_lengths):
    vm = pl.BlockSpec(memory_space=pltpu.VMEM)
    hbm = pl.BlockSpec(memory_space=pl.ANY)
    balance, grad, weight_grad = pl.pallas_call(
        kernel,
        out_shape=(
            jax.ShapeDtypeStruct((1,), F32),
            pltpu.VMEM((TOK, E), F32),
            pltpu.VMEM((ROWS, E), F32),
        ),
        in_specs=[hbm, hbm, hbm, hbm],
        out_specs=(pl.BlockSpec(memory_space=pltpu.SMEM), vm, vm),
        scratch_shapes=scratch(),
        compiler_params=pltpu.CompilerParams(
            collective_id=0, has_side_effects=True, vmem_limit_bytes=60 << 20
        ),
        name="balance_loss",
    )(hidden[0], router_weight, expert_ids[0].T, doc_lengths)
    return balance, grad[None], weight_grad


def solution(mesh):
    placed = (P("win", "ctx", None), P(), P("win", "ctx", None), P("win", None))
    return jax.shard_map(
        shards,
        mesh=mesh,
        in_specs=placed,
        out_specs=(P("win"), P("win", "ctx", None), P(("ctx", "win"), None)),
        check_vma=False,
    )
```

```python
import math

import jax
import jax.numpy as jnp
from jax import lax
from jax.experimental import pallas as pl
from jax.experimental.pallas import tpu as pltpu
from jax.sharding import PartitionSpec as P

MESH = pl.DeviceIdType.MESH
F32 = jnp.float32
BF16 = jnp.bfloat16

D, E, K = 7168, 256, 8
TOK = 1024
DOCS = 64
CTX = 32
LENGTH = TOK * CTX
TCH = 256
NTCH = TOK // TCH
GCH = 256
ROWS = D // 128
RA = 40
RC = ROWS - RA
CHUNK = 16 * ROWS
OFFS = (2, 1, 3)

NPEER = CTX - 1


def split2(v):
    hi = v.astype(BF16)
    lo = (v - hi.astype(F32)).astype(BF16)
    return hi, lo


def sigmoid(v):
    d = jnp.minimum(1.0 + jnp.exp(-v), 8e37)
    r = pl.reciprocal(d, approx=True)
    return r * (2.0 - d * r)


def dot(a, b):
    return jnp.dot(a, b, preferred_element_type=F32)


def loop(n, body, first=0):
    def step(i, carry):
        body(i)
        return carry

    lax.fori_loop(first, n, step, 0)


def kernel(
    hid, wgt, ids_in, lens_in, bal_ref, grad_out, wg_ref,
    ids, lens_ref, xs, ws, picked, share, coef, gbf, loc, dw, crecv,
    pa, pb, pc, arl, brl, crl, ar1, br1, cr1, sa, sb, sc, ar2, br2, cr2, ta, tb, ar3, br3, ar4, br4,
    msg, gat, bmsg, bgat, member2,
    isem, xsem, wsem, gss, grs, bss, brs, css, crs, s1, r1, sz, rz, s2, r2, s3, r3, s4, r4,
):
    ctx = lax.axis_index("ctx")
    y = lax.axis_index("win")
    z, x, c = ctx // 8, (ctx // 2) % 4, ctx % 2

    def at(dz=0, dx=0, dc=0, dy=0):
        return (((z + dz) % 4 * 4 + (x + dx) % 4) * 2 + (c + dc) % 2, (y + dy) % 4)

    def peer(k):
        n = 1 + (k + 19) % NPEER
        return at(n // 8, (n // 2) % 4, n % 2)

    def remote(src, dst, ssem, rsem, where):
        return pltpu.make_async_remote_copy(
            src_ref=src, dst_ref=dst, send_sem=ssem, recv_sem=rsem, device_id=where, device_id_type=MESH
        )

    small = [pltpu.make_async_copy(a, b, isem.at[k]) for k, (a, b) in enumerate(((lens_in, lens_ref), (ids_in, ids)))]
    for cp in small:
        cp.start(priority=0)
    wcopy = pltpu.make_async_copy(wgt, ws, wsem)
    wcopy.start(priority=0)

    def xcopy(t):
        rows = pl.ds(pl.multiple_of(t * TCH, TCH), TCH)
        return pltpu.make_async_copy(hid.at[rows], xs.at[rows], xsem.at[t])

    for t in range(NTCH):
        xcopy(t).start(priority=1)

    barrier = pltpu.get_barrier_semaphore()
    others = [(0, 0, dy) for dy in OFFS] + [(dz, 0, dy) for dz in (1, 3) for dy in OFFS]
    others += [(0, dx, dy) for dx in OFFS for dy in OFFS]

    def greet(k):
        pl.semaphore_signal(barrier, inc=1, device_id=peer(k), device_id_type=MESH)

    loop(NPEER, greet)
    for dz, dx, dy in others:
        pl.semaphore_signal(barrier, inc=1, device_id=at(dz, dx, 0, dy), device_id_type=MESH)
    for cp in small:
        cp.wait()

    lens = jnp.broadcast_to(lens_ref[...].astype(F32), (DOCS, DOCS))
    row = lax.broadcasted_iota(jnp.int32, (DOCS, DOCS), 0)
    col = lax.broadcasted_iota(jnp.int32, (DOCS, DOCS), 1)
    len_c = jnp.sum(jnp.where(row == col, lens, 0.0), axis=1, keepdims=True)
    end_c = jnp.sum(jnp.where(col <= row, lens, 0.0), axis=1, keepdims=True)
    start_c = end_c - len_c
    base = (ctx * TOK).astype(F32)

    def inside(lo, hi, pos):
        return (lo <= pos) & (pos < hi)

    sel_first = inside(start_c, end_c, base)
    sel_last = inside(start_c, end_c, base + (TOK - 1))

    expert = lax.broadcasted_iota(jnp.int32, (E, TCH), 0).astype(F32)

    def choose(t):
        cols = pl.ds(pl.multiple_of(t * TCH, TCH), TCH)
        own = ids[:, cols].astype(F32)
        miss = own[0:1] - expert
        for k in range(1, K):
            miss = miss * (own[k : k + 1] - expert)
        picked[cols, :] = jnp.where(miss == 0.0, 1.0, 0.0).T

    loop(NTCH, choose)

    loc[...] = jnp.zeros_like(loc)

    def forward(t, logits):
        rows = pl.ds(pl.multiple_of(jnp.maximum(t, 0) * TCH, TCH), TCH)
        aff = sigmoid(logits)
        total = jnp.sum(aff, axis=-1, keepdims=True)
        sh = aff * (1.0 / total)
        share[rows, :] = sh
        coef[rows, :] = (float(E) * sh) * (1.0 - aff)
        chosen = picked[rows, :] * aff
        gate = chosen * (1.0 / jnp.sum(chosen, axis=-1, keepdims=True))
        origin = jnp.where(t < 0, -4.0 * LENGTH, base + (t * TCH).astype(F32))
        pos = lax.broadcasted_iota(jnp.int32, (DOCS, TCH), 1).astype(F32) + origin
        mem = jnp.where(inside(start_c, end_c, pos), 1.0, 0.0).astype(BF16)
        loc[...] += dot(mem, jnp.concatenate(split2(gate), axis=1))

    wcopy.wait()

    def ahead(t, logits):
        xcopy(t).wait()
        rows = pl.ds(pl.multiple_of(t * TCH, TCH), TCH)
        new = dot(xs[rows, :], ws[...])
        forward(t - 1, logits)
        return new

    logits = lax.fori_loop(0, NTCH, ahead, jnp.zeros((TCH, E), F32))
    forward(jnp.int32(NTCH - 1), logits)
    local = loc[:, :E] + loc[:, E:]

    first = jnp.sum(jnp.where(sel_first, local, 0.0), axis=0, keepdims=True)
    last = jnp.sum(jnp.where(sel_last, local, 0.0), axis=0, keepdims=True)
    tile = jnp.concatenate(
        [first[:, :128], first[:, 128:], last[:, :128], last[:, 128:], jnp.zeros((4, 128), F32)], axis=0
    )
    msg[...] = tile
    gat[pl.ds(ctx, 1)] = tile[None]

    pl.semaphore_wait(barrier, NPEER + len(others))

    def spread(src, dst, ssem, rsem):
        loop(NPEER, lambda k: remote(src, dst.at[ctx], ssem, rsem, peer(k)).start())

    def everyones(dst, ssem, rsem):
        part = dst.at[pl.ds(0, NPEER)]
        return remote(part, part, ssem, rsem, at(dc=1))

    spread(msg, gat, gss, grs)

    row2 = lax.broadcasted_iota(jnp.int32, (DOCS, 2 * DOCS), 0)
    col2 = lax.broadcasted_iota(jnp.int32, (DOCS, 2 * DOCS), 1) % DOCS
    end_r = jnp.sum(jnp.where(row2 <= col2, len_c, 0.0), axis=0, keepdims=True)
    start_r = jnp.sum(jnp.where(row2 < col2, len_c, 0.0), axis=0, keepdims=True)

    def documents(t):
        rows = pl.ds(pl.multiple_of(t * TCH, TCH), TCH)
        pos = lax.broadcasted_iota(jnp.int32, (TCH, 2 * DOCS), 0).astype(F32) + (base + (t * TCH).astype(F32))
        member2[rows, :] = jnp.where(inside(start_r, end_r, pos), 1.0, 0.0).astype(BF16)

    loop(NTCH, documents)

    gcol = lax.broadcasted_iota(jnp.int32, (2 * DOCS, 8 * CTX), 1)
    grow = lax.broadcasted_iota(jnp.int32, (2 * DOCS, 8 * CTX), 0)
    kind = gcol % 8
    gpos = ((gcol // 8) * TOK).astype(F32)
    start2 = jnp.concatenate([start_c, start_c], axis=0)
    end2 = jnp.concatenate([end_c, end_c], axis=0)
    half = grow // DOCS
    s_first = (kind == half) & inside(start2, end2, gpos)
    s_last = (kind == half + 2) & inside(start2, end2, gpos + (TOK - 1)) & (start2 > gpos)
    smat = jnp.where(s_first | s_last, 1.0, 0.0).astype(BF16)

    everyones(gat, gss, grs).wait_recv()
    ghi, glo = split2(gat[...].reshape(8 * CTX, 128))
    sums = dot(smat, jnp.concatenate([ghi, glo], axis=1))
    sums = sums[:, :128] + sums[:, 128:]
    counts = jnp.concatenate([sums[:DOCS], sums[DOCS:]], axis=1)
    counts = counts + jnp.where(sel_first | sel_last, 0.0, local)
    rates = counts * float(E) / len_c
    rates2 = jnp.concatenate(split2(rates), axis=0)

    def backward(t, gsum):
        rows = pl.ds(pl.multiple_of(t * GCH, GCH), GCH)
        tr = dot(member2[rows, :], rates2)
        mean = jnp.sum(tr * share[rows, :], axis=-1, keepdims=True)
        g = coef[rows, :] * (tr - mean)
        grad_out[rows, :] = g
        gbf[rows, :] = g.astype(BF16)
        return gsum + jnp.sum(mean, axis=0, keepdims=True)

    gsum = lax.fori_loop(0, TOK // GCH, backward, jnp.zeros((1, 1), F32))
    btile = jnp.broadcast_to(gsum, (1, 128))
    bmsg[...] = btile
    bgat[pl.ds(ctx, 1)] = btile[None]

    def ahead_z(q):
        return (2 + 3 * q + 3 * (q // 2) + 2 * (q // 3)) % 4

    other = 1 - x // 2

    def core_copy(i):
        return remote(dw.at[i, :, 1 - c], crecv.at[i], css.at[i], crs.at[i], at(dc=1))

    def second(i):
        zq = (z + ahead_z(i // 2)) % 4
        off = pl.multiple_of(zq * (2 * CHUNK) + (other + i) % 2 * CHUNK, 128)
        prod = lax.dot_general(
            xs[:, pl.ds(off, CHUNK)], gbf[...], (((0,), (0,)), ((), ())), preferred_element_type=F32
        )
        dw[i] = prod.reshape(2, 2, 4 * ROWS, E)
        core_copy(i).start()

    def core_sum(i):
        core_copy(i).wait_recv()
        q = i // 2
        for xi in range(2):
            xd = 2 * ((other + i) % 2) + xi
            v = (dw[i, xi, pl.ds(c, 1)][0] + crecv[i, xi]).reshape(4, ROWS, E)
            pa[q, xd] = v[:, :RA, :128]
            for yd in range(4):
                pb[q, yd, xd] = v[yd, :RA, 128:]
            pc[q, xd] = v[:, RA:, :]

    H0, H1 = pl.ds(0, 2), pl.ds(2, 2)

    def ring(part, q, kind):
        p, rl, r, me = (pa, arl, ar1, x) if part == 0 else (pb, brl, br1, y)
        step = 1 if kind % 2 == 0 else 3
        where = at(dx=step) if part == 0 else at(dy=step)
        opposite, side = (me + 2) % 4, (me + step) % 4
        src, dst = (
            (p.at[q, opposite, H0], rl.at[q, 0]),
            (p.at[q, opposite, H1], rl.at[q, 1]),
            (p.at[q, side, H1], r.at[q, 0, H1]),
            (p.at[q, side, H0], r.at[q, 1, H0]),
            (p.at[q, side, H0], r.at[q, 0, H0]),
            (p.at[q, side, H1], r.at[q, 1, H1]),
        )[kind]
        return remote(src, dst, s1.at[part, q, kind], r1.at[part, q, kind], where)

    def ring_z(kind):
        src, dst = (
            (pc.at[0, H0], crl.at[0]),
            (pc.at[0, H1], crl.at[1]),
            (pc.at[1, H1], cr1.at[0, H1]),
            (pc.at[2, H0], cr1.at[1, H0]),
            (pc.at[1, H0], cr1.at[0, H0]),
            (pc.at[2, H1], cr1.at[1, H1]),
        )[kind]
        return remote(src, dst, sz.at[kind], rz.at[kind], at(dz=1 if kind % 2 == 0 else 3))

    def p1(i):
        q = i // 2
        half = (other + i) % 2

        @pl.when(half == 0)
        def _():
            @pl.when(q == 0)
            def _():
                ring_z(0).start()

            @pl.when(q == 2)
            def _():
                ring_z(3).start()

            ring(1, q, 0).start()
            ring(1, q, 3).start()

        @pl.when(half == 1)
        def _():
            @pl.when(q == 0)
            def _():
                ring_z(1).start()

            @pl.when(q == 1)
            def _():
                ring_z(2).start()

            ring(1, q, 1).start()
            ring(1, q, 2).start()

        @pl.when(i % 2 == 0)
        def _():
            ring(0, q, 0).start()
            ring(0, q, 1).start()

        @pl.when((x + i) % 2 == 0)
        def _():
            ring(0, q, 3).start()

        @pl.when((x + i) % 2 == 1)
        def _():
            ring(0, q, 2).start()

    def p2(q):
        for part in range(2):
            p, rl, me = ((pa, arl, x), (pb, brl, y))[part]
            for d, (step, h) in enumerate(((1, H0), (3, H1))):
                ring(part, q, d).wait_recv()
                side = (me + step) % 4
                p[q, pl.ds(side, 1), h] = p[q, pl.ds(side, 1), h] + rl[q, pl.ds(d, 1)]
                ring(part, q, 4 + d).start()

    def p2_z():
        ring_z(0).wait_recv()
        pc[1, H0] = pc[1, H0] + crl[0]
        ring_z(4).start()
        ring_z(1).wait_recv()
        pc[2, H1] = pc[2, H1] + crl[1]
        ring_z(5).start()

    def a2(q, k):
        return remote(sa.at[q, (y + OFFS[k]) % 4], ar2.at[q, k], s2.at[0, q, k], r2.at[0, q, k], at(dy=OFFS[k]))

    def b2(q):
        return remote(sb.at[q], br2.at[q], s2.at[1, q, 0], r2.at[1, q, 0], at(dz=ahead_z(q)))

    def c2(k):
        n = 1 + (k + 9) % 15
        dx, dy = n // 4, n % 4
        return remote(sc.at[(x + dx) % 4, (y + dy) % 4], cr2.at[n - 1], s2.at[1, 3, 0], r2.at[1, 3, 0], at(dx=dx, dy=dy))

    def c2_all():
        part = cr2.at[pl.ds(0, 15)]
        return remote(part, part, s2.at[1, 3, 0], r2.at[1, 3, 0], at(dc=1))

    def a23(k):
        return remote(sa.at[2, (y + k) % 4], ar4.at[k], s4.at[0, k], r4.at[0, k], at(dz=3, dy=k))

    def b23(k):
        return remote(sb.at[2, (x + k) % 4], br4.at[k], s4.at[1, k], r4.at[1, k], at(dz=3, dx=k))

    def a3(q):
        return remote(ta.at[q], ar3.at[q], s3.at[0, q], r3.at[0, q], at(dz=ahead_z(q)))

    def b3(k):
        return remote(tb.at[(x + OFFS[k]) % 4], br3.at[k], s3.at[1, k], r3.at[1, k], at(dx=OFFS[k]))

    def p3(q):
        for kind in range(2, 6):
            ring(0, q, kind).wait_recv()
        sa[q] = pa[q, pl.ds(x, 1)][0] + ar1[q, 0] + ar1[q, 1]

        @pl.when(q == 2)
        def _():
            for k in (2, 1, 3, 0):
                a23(k).start()

        @pl.when(q != 2)
        def _():
            for k in range(3):
                a2(q, k).start()

        for kind in range(2, 6):
            ring(1, q, kind).wait_recv()
        sb[q] = pb[q, pl.ds(y, 1)][0] + br1[q, 0] + br1[q, 1]

        @pl.when(q < 2)
        def _():
            b2(q).start()

        @pl.when(q == 2)
        def _():
            for k in (2, 1, 3, 0):
                b23(k).start()

        for kind in range(4):
            ring(0, q, kind).wait_send()
            ring(1, q, kind).wait_send()

    def p4(q):
        for k in range(3):
            a2(q, k).wait_recv()
        ta[q] = sa[q, pl.ds(y, 1)][0] + ar2[q, 0] + ar2[q, 1] + ar2[q, 2]

        @pl.when(q < 2)
        def _():
            a3(q).start()

    def slot(i):
        @pl.when(i < 8)
        def _():
            second(i)

        @pl.when((i >= 2) & (i < 10))
        def _():
            core_sum(i - 2)
            p1(i - 2)

        @pl.when(i == 10)
        def _():
            spread(bmsg, bgat, bss, brs)

        @pl.when((i >= 9) & (i < 11))
        def _():
            p3(i - 9)

        @pl.when((i >= 5) & (i < 12) & (i % 2 == 1))
        def _():
            p2((i - 5) // 2)

        @pl.when(i == 7)
        def _():
            p2_z()

        @pl.when(i == 11)
        def _():
            for kind in range(2, 6):
                ring_z(kind).wait_recv()
            sc[...] = pc[3] + cr1[0] + cr1[1]
            loop(15, lambda k: c2(k).start())

        @pl.when((i >= 11) & (i < 13))
        def _():
            p3(i - 9)

        @pl.when(i == 12)
        def _():
            for q in range(2):
                b2(q).wait_recv()
            tb[...] = sb[3] + br2[0] + br2[1]
            for k in range(3):
                b3(k).start()

        @pl.when(i >= 11)
        def _():
            p4((i - 11) + (i // 13))

    loop(14, slot)

    everyones(bgat, bss, brs).wait_recv()
    bal = jnp.sum(bgat[...], axis=0) * (1.0 / LENGTH)
    bal_ref[0] = bal[0, 0]
    loop(8, lambda i: core_copy(i).wait_send())
    everyones(gat, gss, grs).wait_send()
    everyones(bgat, bss, brs).wait_send()
    for kind in range(6):
        ring_z(kind).wait_send()

    def ring_sent(q):
        for kind in range(4, 6):
            ring(0, q, kind).wait_send()
            ring(1, q, kind).wait_send()

    loop(4, ring_sent)
    scale = 1.0 / math.sqrt(LENGTH * 4)
    c2_all().wait_recv()
    own_c = sc[pl.ds(x, 1), pl.ds(y, 1)].reshape(RC, E)
    wg_ref[RA:, :] = (own_c + jnp.sum(cr2[...], axis=0)) * scale
    for k in range(2):
        a3(k).wait_recv()
    for k in range(4):
        a23(k).wait_recv()
    wg_ref[:RA, :128] = (ta[3] + ar3[0] + ar3[1] + ((ar4[0] + ar4[1]) + (ar4[2] + ar4[3]))) * scale
    for k in range(4):
        b23(k).wait_recv()
    for k in range(3):
        b3(k).wait_recv()
    own_b = tb[pl.ds(x, 1)][0] + br3[0] + br3[1] + br3[2]
    wg_ref[:RA, 128:] = (own_b + ((br4[0] + br4[1]) + (br4[2] + br4[3]))) * scale
    for k in range(3):
        for q in (0, 1, 3):
            a2(q, k).wait_send()
        b3(k).wait_send()
    for k in range(2):
        b2(k).wait_send()
        a3(k).wait_send()
    for k in range(4):
        a23(k).wait_send()
        b23(k).wait_send()
    c2_all().wait_send()


def scratch():
    v = pltpu.VMEM
    s = pltpu.SemaphoreType.DMA
    return [
        v((K, TOK), jnp.int32), v((1, DOCS), jnp.int32),
        v((TOK, D), BF16), v((D, E), BF16), v((TOK, E), F32), v((TOK, E), F32), v((TOK, E), F32),
        v((TOK, E), BF16), v((DOCS, 2 * E), F32),
        v((8, 2, 2, 4 * ROWS, E), F32), v((8, 2, 4 * ROWS, E), F32),
        v((4, 4, 4, RA, 128), F32), v((4, 4, 4, RA, 128), F32), v((4, 4, 4, RC, E), F32),
        v((4, 2, 2, RA, 128), F32), v((4, 2, 2, RA, 128), F32), v((2, 2, 4, RC, E), F32),
        v((4, 2, 4, RA, 128), F32), v((4, 2, 4, RA, 128), F32), v((2, 4, 4, RC, E), F32),
        v((4, 4, RA, 128), F32), v((4, 4, RA, 128), F32), v((4, 4, RC, E), F32),
        v((4, 3, RA, 128), F32), v((2, 4, RA, 128), F32), v((15, RC, E), F32),
        v((4, RA, 128), F32), v((4, RA, 128), F32),
        v((2, RA, 128), F32), v((3, RA, 128), F32), v((4, RA, 128), F32), v((4, RA, 128), F32),
        v((8, 128), F32), v((CTX, 8, 128), F32), v((1, 128), F32), v((CTX, 1, 128), F32), v((TOK, 2 * DOCS), BF16),
        s((2,)), s((NTCH,)), s, s, s, s, s, s((8,)), s((8,)),
        s((2, 4, 6)), s((2, 4, 6)), s((6,)), s((6,)), s((2, 4, 3)), s((2, 4, 3)), s((3, 3)), s((3, 3)), s((2, 4)), s((2, 4)),
    ]


def shards(hidden, router_weight, expert_ids, doc_lengths):
    vm = pl.BlockSpec(memory_space=pltpu.VMEM)
    hbm = pl.BlockSpec(memory_space=pl.ANY)
    balance, grad, weight_grad = pl.pallas_call(
        kernel,
        out_shape=(
            jax.ShapeDtypeStruct((1,), F32),
            pltpu.VMEM((TOK, E), F32),
            pltpu.VMEM((ROWS, E), F32),
        ),
        in_specs=[hbm, hbm, hbm, hbm],
        out_specs=(pl.BlockSpec(memory_space=pltpu.SMEM), vm, vm),
        scratch_shapes=scratch(),
        compiler_params=pltpu.CompilerParams(
            collective_id=0, has_side_effects=True, vmem_limit_bytes=60 << 20
        ),
        name="balance_loss",
    )(hidden[0], router_weight, expert_ids[0].T, doc_lengths)
    return balance, grad[None], weight_grad


def solution(mesh):
    placed = (P("win", "ctx", None), P(), P("win", "ctx", None), P("win", None))
    return jax.shard_map(
        shards,
        mesh=mesh,
        in_specs=placed,
        out_specs=(P("win"), P("win", "ctx", None), P(("ctx", "win"), None)),
        check_vma=False,
    )
```

```python
import math

import jax
import jax.numpy as jnp
from jax import lax
from jax.experimental import pallas as pl
from jax.experimental.pallas import tpu as pltpu
from jax.sharding import PartitionSpec as P

MESH = pl.DeviceIdType.MESH
F32 = jnp.float32
BF16 = jnp.bfloat16

D, E, K = 7168, 256, 8
TOK = 1024
DOCS = 64
CTX = 32
LENGTH = TOK * CTX
TCH = 256
NTCH = TOK // TCH
GCH = 1024
ROWS = D // 128
RA = 40
RC = ROWS - RA
CHUNK = 16 * ROWS
OFFS = (2, 1, 3)

NPEER = CTX - 1


def split2(v):
    hi = v.astype(BF16)
    lo = (v - hi.astype(F32)).astype(BF16)
    return hi, lo


def sigmoid(v):
    d = jnp.minimum(1.0 + jnp.exp(-v), 8e37)
    r = pl.reciprocal(d, approx=True)
    return r * (2.0 - d * r)


def dot(a, b):
    return jnp.dot(a, b, preferred_element_type=F32)


def loop(n, body, first=0):
    def step(i, carry):
        body(i)
        return carry

    lax.fori_loop(first, n, step, 0)


def kernel(
    hid, wgt, ids_in, lens_in, bal_ref, grad_out, wg_ref,
    ids, lens_ref, xs, ws, picked, share, coef, gbf, loc, dw, crecv,
    pa, pb, pc, arl, brl, crl, ar1, br1, cr1, sa, sb, sc, ar2, br2, cr2, ta, tb, ar3, br3, ar4, br4,
    msg, gat, bmsg, bgat, member2,
    isem, xsem, wsem, gss, grs, bss, brs, css, crs, s1, r1, sz, rz, s2, r2, s3, r3, s4, r4,
):
    ctx = lax.axis_index("ctx")
    y = lax.axis_index("win")
    z, x, c = lax.div(ctx, 8), lax.rem(lax.div(ctx, 2), 4), lax.rem(ctx, 2)

    nz, nx, ny = ([v] + [lax.rem(v + o, 4) for o in (1, 2, 3)] for v in (z, x, y))

    def along(near, o):
        return near[o] if isinstance(o, int) else lax.rem(near[0] + o, 4)

    def at(dz=0, dx=0, dc=0, dy=0):
        core = c if isinstance(dc, int) and dc == 0 else lax.rem(c + dc, 2)
        return ((along(nz, dz) * 4 + along(nx, dx)) * 2 + core, along(ny, dy))

    def peer(n):
        return at(lax.div(n, 8), lax.rem(lax.div(n, 2), 4), lax.rem(n, 2))

    def peers(body):
        loop(CTX, body, 20)
        loop(20, body, 1)

    def remote(src, dst, ssem, rsem, where):
        return pltpu.make_async_remote_copy(
            src_ref=src, dst_ref=dst, send_sem=ssem, recv_sem=rsem, device_id=where, device_id_type=MESH
        )

    small = [pltpu.make_async_copy(a, b, isem.at[k]) for k, (a, b) in enumerate(((lens_in, lens_ref), (ids_in, ids)))]
    for cp in small:
        cp.start(priority=0)
    wcopy = pltpu.make_async_copy(wgt, ws, wsem)
    wcopy.start(priority=0)

    def xcopy(t):
        rows = pl.ds(pl.multiple_of(t * TCH, TCH), TCH)
        return pltpu.make_async_copy(hid.at[rows], xs.at[rows], xsem.at[t])

    for t in range(NTCH):
        xcopy(t).start(priority=1)

    barrier = pltpu.get_barrier_semaphore()
    others = [(0, 0, dy) for dy in OFFS] + [(dz, 0, dy) for dz in (1, 3) for dy in OFFS]
    others += [(0, dx, dy) for dx in OFFS for dy in OFFS]

    def greet(n):
        pl.semaphore_signal(barrier, inc=1, device_id=peer(n), device_id_type=MESH)

    peers(greet)
    for dz, dx, dy in others:
        pl.semaphore_signal(barrier, inc=1, device_id=at(dz, dx, 0, dy), device_id_type=MESH)
    for cp in small:
        cp.wait()

    lens = jnp.broadcast_to(lens_ref[...].astype(F32), (DOCS, DOCS))
    row = lax.broadcasted_iota(jnp.int32, (DOCS, DOCS), 0)
    col = lax.broadcasted_iota(jnp.int32, (DOCS, DOCS), 1)
    len_c = jnp.sum(jnp.where(row == col, lens, 0.0), axis=1, keepdims=True)
    end_c = jnp.sum(jnp.where(col <= row, lens, 0.0), axis=1, keepdims=True)
    start_c = end_c - len_c
    base = (ctx * TOK).astype(F32)

    def inside(lo, hi, pos):
        return (lo <= pos) & (pos < hi)

    sel_first = inside(start_c, end_c, base)
    sel_last = inside(start_c, end_c, base + (TOK - 1))

    expert = lax.broadcasted_iota(jnp.int32, (E, TCH), 0).astype(F32)

    def choose(t):
        cols = pl.ds(pl.multiple_of(t * TCH, TCH), TCH)
        own = ids[:, cols].astype(F32)
        miss = own[0:1] - expert
        for k in range(1, K):
            miss = miss * (own[k : k + 1] - expert)
        picked[cols, :] = jnp.where(miss == 0.0, 1.0, 0.0).T

    loop(NTCH, choose)

    loc[...] = jnp.zeros_like(loc)

    def forward(t, logits):
        rows = pl.ds(pl.multiple_of(jnp.maximum(t, 0) * TCH, TCH), TCH)
        aff = sigmoid(logits)
        total = jnp.sum(aff, axis=-1, keepdims=True)
        sh = aff * (1.0 / total)
        share[rows, :] = sh
        coef[rows, :] = (float(E) * sh) * (1.0 - aff)
        chosen = picked[rows, :] * aff
        gate = chosen * (1.0 / jnp.sum(chosen, axis=-1, keepdims=True))
        origin = jnp.where(t < 0, -4.0 * LENGTH, base + (t * TCH).astype(F32))
        pos = lax.broadcasted_iota(jnp.int32, (DOCS, TCH), 1).astype(F32) + origin
        mem = jnp.where(inside(start_c, end_c, pos), 1.0, 0.0).astype(BF16)
        loc[...] += dot(mem, jnp.concatenate(split2(gate), axis=1))

    wcopy.wait()

    def ahead(t, logits):
        xcopy(t).wait()
        rows = pl.ds(pl.multiple_of(t * TCH, TCH), TCH)
        new = dot(xs[rows, :], ws[...])
        forward(t - 1, logits)
        return new

    logits = lax.fori_loop(0, NTCH, ahead, jnp.zeros((TCH, E), F32))
    forward(jnp.int32(NTCH - 1), logits)
    local = loc[:, :E] + loc[:, E:]

    first = jnp.sum(jnp.where(sel_first, local, 0.0), axis=0, keepdims=True)
    last = jnp.sum(jnp.where(sel_last, local, 0.0), axis=0, keepdims=True)
    tile = jnp.concatenate([first[:, :128], first[:, 128:], last[:, :128], last[:, 128:]], axis=0)
    msg[...] = tile
    gat[pl.ds(ctx, 1)] = tile[None]

    pl.semaphore_wait(barrier, NPEER + len(others))

    def spread(src, dst, ssem, rsem):
        peers(lambda n: remote(src, dst.at[ctx], ssem, rsem, peer(n)).start())

    def everyones(dst, ssem, rsem):
        part = dst.at[pl.ds(0, NPEER)]
        return remote(part, part, ssem, rsem, at(dc=1))

    spread(msg, gat, gss, grs)

    row2 = lax.broadcasted_iota(jnp.int32, (DOCS, 2 * DOCS), 0)
    col2 = lax.broadcasted_iota(jnp.int32, (DOCS, 2 * DOCS), 1) % DOCS
    end_r = jnp.sum(jnp.where(row2 <= col2, len_c, 0.0), axis=0, keepdims=True)
    start_r = jnp.sum(jnp.where(row2 < col2, len_c, 0.0), axis=0, keepdims=True)

    def documents(t):
        rows = pl.ds(pl.multiple_of(t * TCH, TCH), TCH)
        pos = lax.broadcasted_iota(jnp.int32, (TCH, 2 * DOCS), 0).astype(F32) + (base + (t * TCH).astype(F32))
        member2[rows, :] = jnp.where(inside(start_r, end_r, pos), 1.0, 0.0).astype(BF16)

    loop(NTCH, documents)

    gcol = lax.broadcasted_iota(jnp.int32, (2 * DOCS, 8 * CTX), 1)
    grow = lax.broadcasted_iota(jnp.int32, (2 * DOCS, 8 * CTX), 0)
    kind = gcol % 8
    gpos = ((gcol // 8) * TOK).astype(F32)
    start2 = jnp.concatenate([start_c, start_c], axis=0)
    end2 = jnp.concatenate([end_c, end_c], axis=0)
    half = grow // DOCS
    s_first = (kind == half) & inside(start2, end2, gpos)
    s_last = (kind == half + 2) & inside(start2, end2, gpos + (TOK - 1)) & (start2 > gpos)
    smat = jnp.where(s_first | s_last, 1.0, 0.0).astype(BF16)

    everyones(gat, gss, grs).wait_recv()
    ghi, glo = split2(jnp.concatenate([gat[...], jnp.zeros((CTX, 4, 128), F32)], axis=1).reshape(8 * CTX, 128))
    sums = dot(smat, jnp.concatenate([ghi, glo], axis=1))
    sums = sums[:, :128] + sums[:, 128:]
    counts = jnp.concatenate([sums[:DOCS], sums[DOCS:]], axis=1)
    counts = counts + jnp.where(sel_first | sel_last, 0.0, local)
    rates = counts * float(E) / len_c
    rates2 = jnp.concatenate(split2(rates), axis=0)

    def backward(t, gsum):
        rows = pl.ds(pl.multiple_of(t * GCH, GCH), GCH)
        tr = dot(member2[rows, :], rates2)
        mean = jnp.sum(tr * share[rows, :], axis=-1, keepdims=True)
        g = coef[rows, :] * (tr - mean)
        grad_out[rows, :] = g
        gbf[rows, :] = g.astype(BF16)
        return gsum + jnp.sum(mean, axis=0, keepdims=True)

    gsum = lax.fori_loop(0, TOK // GCH, backward, jnp.zeros((1, 1), F32))
    btile = jnp.broadcast_to(gsum, (1, 128))
    bmsg[...] = btile
    bgat[pl.ds(ctx, 1)] = btile[None]

    def ahead_z(q):
        return lax.rem(2 + 3 * q + 3 * lax.div(q, 2) + 2 * lax.div(q, 3), 4)

    other = 1 - lax.div(x, 2)

    def core_copy(i):
        return remote(dw.at[i, :, 1 - c], crecv.at[i], css.at[i], crs.at[i], at(dc=1))

    def second(i):
        zq = lax.rem(z + ahead_z(lax.div(i, 2)), 4)
        off = pl.multiple_of(zq * (2 * CHUNK) + lax.rem(other + i, 2) * CHUNK, 128)
        prod = lax.dot_general(
            xs[:, pl.ds(off, CHUNK)], gbf[...], (((0,), (0,)), ((), ())), preferred_element_type=F32
        )
        dw[i] = prod.reshape(2, 2, 4 * ROWS, E)
        core_copy(i).start()

    def core_sum(i):
        core_copy(i).wait_recv()
        q = lax.div(i, 2)
        for xi in range(2):
            xd = 2 * lax.rem(other + i, 2) + xi
            v = (dw[i, xi, pl.ds(c, 1)][0] + crecv[i, xi]).reshape(4, ROWS, E)
            pa[q, xd] = v[:, :RA, :128]
            for yd in range(4):
                pb[q, yd, xd] = v[yd, :RA, 128:]
            pc[q, xd] = v[:, RA:, :]

    H0, H1 = pl.ds(0, 2), pl.ds(2, 2)

    def ring(part, q, kind):
        p, rl, r, near = (pa, arl, ar1, nx) if part == 0 else (pb, brl, br1, ny)
        step = 1 if kind % 2 == 0 else 3
        where = at(dx=step) if part == 0 else at(dy=step)
        opposite, side = near[2], near[step]
        src, dst = (
            (p.at[q, opposite, H0], rl.at[q, 0]),
            (p.at[q, opposite, H1], rl.at[q, 1]),
            (p.at[q, side, H1], r.at[q, 0, H1]),
            (p.at[q, side, H0], r.at[q, 1, H0]),
            (p.at[q, side, H0], r.at[q, 0, H0]),
            (p.at[q, side, H1], r.at[q, 1, H1]),
        )[kind]
        return remote(src, dst, s1.at[part, q, kind], r1.at[part, q, kind], where)

    def ring_z(kind):
        src, dst = (
            (pc.at[0, H0], crl.at[0]),
            (pc.at[0, H1], crl.at[1]),
            (pc.at[1, H1], cr1.at[0, H1]),
            (pc.at[2, H0], cr1.at[1, H0]),
            (pc.at[1, H0], cr1.at[0, H0]),
            (pc.at[2, H1], cr1.at[1, H1]),
        )[kind]
        return remote(src, dst, sz.at[kind], rz.at[kind], at(dz=1 if kind % 2 == 0 else 3))

    def p1(i):
        q = lax.div(i, 2)
        half = lax.rem(other + i, 2)

        @pl.when(half == 0)
        def _():
            @pl.when(q == 0)
            def _():
                ring_z(0).start()

            @pl.when(q == 2)
            def _():
                ring_z(3).start()

            ring(1, q, 0).start()
            ring(1, q, 3).start()

        @pl.when(half == 1)
        def _():
            @pl.when(q == 0)
            def _():
                ring_z(1).start()

            @pl.when(q == 1)
            def _():
                ring_z(2).start()

            ring(1, q, 1).start()
            ring(1, q, 2).start()

        @pl.when(lax.rem(i, 2) == 0)
        def _():
            ring(0, q, 0).start()
            ring(0, q, 1).start()

        @pl.when(lax.rem(x + i, 2) == 0)
        def _():
            ring(0, q, 3).start()

        @pl.when(lax.rem(x + i, 2) == 1)
        def _():
            ring(0, q, 2).start()

    def p2(q):
        for part in range(2):
            p, rl, near = ((pa, arl, nx), (pb, brl, ny))[part]
            for d, (step, h) in enumerate(((1, H0), (3, H1))):
                ring(part, q, d).wait_recv()
                side = near[step]
                p[q, pl.ds(side, 1), h] = p[q, pl.ds(side, 1), h] + rl[q, pl.ds(d, 1)]
                ring(part, q, 4 + d).start()

    def p2_z():
        ring_z(0).wait_recv()
        pc[1, H0] = pc[1, H0] + crl[0]
        ring_z(4).start()
        ring_z(1).wait_recv()
        pc[2, H1] = pc[2, H1] + crl[1]
        ring_z(5).start()

    def a2(q, k):
        return remote(sa.at[q, ny[OFFS[k]]], ar2.at[q, k], s2.at[0, q, k], r2.at[0, q, k], at(dy=OFFS[k]))

    def b2(q):
        q = jnp.int32(q)
        return remote(sb.at[q], br2.at[q], s2.at[1, q, 0], r2.at[1, q, 0], at(dz=ahead_z(q)))

    def c2(k):
        n = 1 + lax.rem(k + 9, 15)
        dx, dy = lax.div(n, 4), lax.rem(n, 4)
        return remote(sc.at[along(nx, dx), along(ny, dy)], cr2.at[n - 1], s2.at[1, 3, 0], r2.at[1, 3, 0], at(dx=dx, dy=dy))

    def c2_all():
        part = cr2.at[pl.ds(0, 15)]
        return remote(part, part, s2.at[1, 3, 0], r2.at[1, 3, 0], at(dc=1))

    def a23(k):
        return remote(sa.at[2, ny[k]], ar4.at[k], s4.at[0, k], r4.at[0, k], at(dz=3, dy=k))

    def b23(k):
        return remote(sb.at[2, nx[k]], br4.at[k], s4.at[1, k], r4.at[1, k], at(dz=3, dx=k))

    def a3(q):
        q = jnp.int32(q)
        return remote(ta.at[q], ar3.at[q], s3.at[0, q], r3.at[0, q], at(dz=ahead_z(q)))

    def b3(k):
        return remote(tb.at[nx[OFFS[k]]], br3.at[k], s3.at[1, k], r3.at[1, k], at(dx=OFFS[k]))

    def p3(q):
        for kind in range(2, 6):
            ring(0, q, kind).wait_recv()
        sa[q] = pa[q, pl.ds(x, 1)][0] + ar1[q, 0] + ar1[q, 1]

        @pl.when(q == 2)
        def _():
            for k in (2, 1, 3, 0):
                a23(k).start()

        @pl.when(q != 2)
        def _():
            for k in range(3):
                a2(q, k).start()

        for kind in range(2, 6):
            ring(1, q, kind).wait_recv()
        sb[q] = pb[q, pl.ds(y, 1)][0] + br1[q, 0] + br1[q, 1]

        @pl.when(q < 2)
        def _():
            b2(q).start()

        @pl.when(q == 2)
        def _():
            for k in (2, 1, 3, 0):
                b23(k).start()

        for kind in range(4):
            ring(0, q, kind).wait_send()
            ring(1, q, kind).wait_send()

    def p4(q):
        for k in range(3):
            a2(q, k).wait_recv()
        ta[q] = sa[q, pl.ds(y, 1)][0] + ar2[q, 0] + ar2[q, 1] + ar2[q, 2]

        @pl.when(q < 2)
        def _():
            a3(q).start()

    def slot(i):
        @pl.when(i < 8)
        def _():
            second(i)

        @pl.when((i >= 2) & (i < 10))
        def _():
            core_sum(i - 2)
            p1(i - 2)

        @pl.when(i == 10)
        def _():
            spread(bmsg, bgat, bss, brs)

        @pl.when((i >= 9) & (i < 11))
        def _():
            p3(i - 9)

        @pl.when((i >= 5) & (i < 12) & (lax.rem(i, 2) == 1))
        def _():
            p2(lax.div(i - 5, 2))

        @pl.when(i == 7)
        def _():
            p2_z()

        @pl.when(i == 11)
        def _():
            for kind in range(2, 6):
                ring_z(kind).wait_recv()
            sc[...] = pc[3] + cr1[0] + cr1[1]
            loop(15, lambda k: c2(k).start())

        @pl.when((i >= 11) & (i < 13))
        def _():
            p3(i - 9)

        @pl.when(i == 12)
        def _():
            for q in range(2):
                b2(q).wait_recv()
            tb[...] = sb[3] + br2[0] + br2[1]
            for k in range(3):
                b3(k).start()

        @pl.when(i >= 11)
        def _():
            p4(i - 11 + lax.div(i, 13))

    loop(14, slot)

    everyones(bgat, bss, brs).wait_recv()
    bal = jnp.sum(bgat[...], axis=0) * (1.0 / LENGTH)
    bal_ref[0] = bal[0, 0]
    loop(8, lambda i: core_copy(i).wait_send())
    everyones(gat, gss, grs).wait_send()
    everyones(bgat, bss, brs).wait_send()
    for kind in range(6):
        ring_z(kind).wait_send()

    def ring_sent(q):
        for kind in range(4, 6):
            ring(0, q, kind).wait_send()
            ring(1, q, kind).wait_send()

    loop(4, ring_sent)
    scale = 1.0 / math.sqrt(LENGTH * 4)
    c2_all().wait_recv()
    own_c = sc[pl.ds(x, 1), pl.ds(y, 1)].reshape(RC, E)
    wg_ref[RA:, :] = (own_c + jnp.sum(cr2[...], axis=0)) * scale
    for k in range(2):
        a3(k).wait_recv()
    for k in range(4):
        a23(k).wait_recv()
    wg_ref[:RA, :128] = (ta[3] + ar3[0] + ar3[1] + ((ar4[0] + ar4[1]) + (ar4[2] + ar4[3]))) * scale
    for k in range(4):
        b23(k).wait_recv()
    for k in range(3):
        b3(k).wait_recv()
    own_b = tb[pl.ds(x, 1)][0] + br3[0] + br3[1] + br3[2]
    wg_ref[:RA, 128:] = (own_b + ((br4[0] + br4[1]) + (br4[2] + br4[3]))) * scale
    for k in range(3):
        for q in (0, 1, 3):
            a2(q, k).wait_send()
        b3(k).wait_send()
    for k in range(2):
        b2(k).wait_send()
        a3(k).wait_send()
    for k in range(4):
        a23(k).wait_send()
        b23(k).wait_send()
    c2_all().wait_send()


def scratch():
    v = pltpu.VMEM
    s = pltpu.SemaphoreType.DMA
    return [
        v((K, TOK), jnp.int32), v((1, DOCS), jnp.int32),
        v((TOK, D), BF16), v((D, E), BF16), v((TOK, E), F32), v((TOK, E), F32), v((TOK, E), F32),
        v((TOK, E), BF16), v((DOCS, 2 * E), F32),
        v((8, 2, 2, 4 * ROWS, E), F32), v((8, 2, 4 * ROWS, E), F32),
        v((4, 4, 4, RA, 128), F32), v((4, 4, 4, RA, 128), F32), v((4, 4, 4, RC, E), F32),
        v((4, 2, 2, RA, 128), F32), v((4, 2, 2, RA, 128), F32), v((2, 2, 4, RC, E), F32),
        v((4, 2, 4, RA, 128), F32), v((4, 2, 4, RA, 128), F32), v((2, 4, 4, RC, E), F32),
        v((4, 4, RA, 128), F32), v((4, 4, RA, 128), F32), v((4, 4, RC, E), F32),
        v((4, 3, RA, 128), F32), v((2, 4, RA, 128), F32), v((15, RC, E), F32),
        v((4, RA, 128), F32), v((4, RA, 128), F32),
        v((2, RA, 128), F32), v((3, RA, 128), F32), v((4, RA, 128), F32), v((4, RA, 128), F32),
        v((4, 128), F32), v((CTX, 4, 128), F32), v((1, 128), F32), v((CTX, 1, 128), F32), v((TOK, 2 * DOCS), BF16),
        s((2,)), s((NTCH,)), s, s, s, s, s, s((8,)), s((8,)),
        s((2, 4, 6)), s((2, 4, 6)), s((6,)), s((6,)), s((2, 4, 3)), s((2, 4, 3)), s((3, 3)), s((3, 3)), s((2, 4)), s((2, 4)),
    ]


def shards(hidden, router_weight, expert_ids, doc_lengths):
    vm = pl.BlockSpec(memory_space=pltpu.VMEM)
    hbm = pl.BlockSpec(memory_space=pl.ANY)
    balance, grad, weight_grad = pl.pallas_call(
        kernel,
        out_shape=(
            pltpu.SMEM((1,), F32),
            pltpu.VMEM((TOK, E), F32),
            pltpu.VMEM((ROWS, E), F32),
        ),
        in_specs=[hbm, hbm, hbm, hbm],
        out_specs=(pl.BlockSpec(memory_space=pltpu.SMEM), vm, vm),
        scratch_shapes=scratch(),
        compiler_params=pltpu.CompilerParams(
            collective_id=0, has_side_effects=True, vmem_limit_bytes=60 << 20
        ),
        name="balance_loss",
    )(hidden[0], router_weight, expert_ids[0].T, doc_lengths)
    return balance, grad[None], weight_grad


def solution(mesh):
    placed = (P("win", "ctx", None), P(), P("win", "ctx", None), P("win", None))
    return jax.shard_map(
        shards,
        mesh=mesh,
        in_specs=placed,
        out_specs=(P("win"), P("win", "ctx", None), P(("ctx", "win"), None)),
        check_vma=False,
    )
```

```python
import math

import jax
import jax.numpy as jnp
from jax import lax
from jax.experimental import pallas as pl
from jax.experimental.pallas import tpu as pltpu
from jax.sharding import PartitionSpec as P

MESH = pl.DeviceIdType.MESH
F32 = jnp.float32
BF16 = jnp.bfloat16

D, E, K = 7168, 256, 8
TOK = 1024
DOCS = 64
CTX = 32
LENGTH = TOK * CTX
TCH = 256
NTCH = TOK // TCH
GCH = 1024
ROWS = D // 128
RA = 40
RC = ROWS - RA
CHUNK = 16 * ROWS
OFFS = (2, 1, 3)

NPEER = CTX - 1


def split2(v):
    hi = v.astype(BF16)
    lo = (v - hi.astype(F32)).astype(BF16)
    return hi, lo


def sigmoid(v):
    d = jnp.minimum(1.0 + jnp.exp(-v), 8e37)
    r = pl.reciprocal(d, approx=True)
    return r * (2.0 - d * r)


def dot(a, b):
    return jnp.dot(a, b, preferred_element_type=F32)


def loop(n, body, first=0):
    def step(i, carry):
        body(i)
        return carry

    lax.fori_loop(first, n, step, 0)


def kernel(
    hid, wgt, ids_in, lens_in, bal_ref, grad_out, wg_ref,
    ids, lens_ref, xs, ws, picked, share, coef, gbf, loc, dw, crecv,
    pa, pb, pc, arl, brl, crl, ar1, br1, cr1, sa, sb, sc, ar2, br2, cr2, ta, tb, ar3, br3, ar4, br4,
    msg, gat, bmsg, bgat, member2,
    isem, xsem, wsem, gss, grs, bss, brs, css, crs, s1, r1, sz, rz, s2, r2, s3, r3, s4, r4,
):
    ctx = lax.axis_index("ctx")
    y = lax.axis_index("win")
    z, x, c = lax.div(ctx, 8), lax.rem(lax.div(ctx, 2), 4), lax.rem(ctx, 2)

    nz, nx, ny = ([v] + [lax.rem(v + o, 4) for o in (1, 2, 3)] for v in (z, x, y))

    def along(near, o):
        return near[o] if isinstance(o, int) else lax.rem(near[0] + o, 4)

    def at(dz=0, dx=0, dc=0, dy=0):
        core = c if isinstance(dc, int) and dc == 0 else lax.rem(c + dc, 2)
        return ((along(nz, dz) * 4 + along(nx, dx)) * 2 + core, along(ny, dy))

    def peer(n):
        return at(lax.div(n, 8), lax.rem(lax.div(n, 2), 4), lax.rem(n, 2))

    def peers(body):
        loop(CTX, body, 20)
        loop(20, body, 1)

    def remote(src, dst, ssem, rsem, where):
        return pltpu.make_async_remote_copy(
            src_ref=src, dst_ref=dst, send_sem=ssem, recv_sem=rsem, device_id=where, device_id_type=MESH
        )

    small = [pltpu.make_async_copy(a, b, isem.at[k]) for k, (a, b) in enumerate(((lens_in, lens_ref), (ids_in, ids)))]
    for cp in small:
        cp.start(priority=0)
    wcopy = pltpu.make_async_copy(wgt, ws, wsem)
    wcopy.start(priority=0)

    def xcopy(t):
        rows = pl.ds(pl.multiple_of(t * TCH, TCH), TCH)
        return pltpu.make_async_copy(hid.at[rows], xs.at[rows], xsem.at[t])

    for t in range(NTCH):
        xcopy(t).start(priority=1)

    barrier = pltpu.get_barrier_semaphore()
    others = [(0, 0, dy) for dy in OFFS] + [(dz, 0, dy) for dz in (1, 3) for dy in OFFS]
    others += [(0, dx, dy) for dx in OFFS for dy in OFFS]

    def greet(n):
        pl.semaphore_signal(barrier, inc=1, device_id=peer(n), device_id_type=MESH)

    peers(greet)
    for dz, dx, dy in others:
        pl.semaphore_signal(barrier, inc=1, device_id=at(dz, dx, 0, dy), device_id_type=MESH)
    for cp in small:
        cp.wait()

    lens = jnp.broadcast_to(lens_ref[...].astype(F32), (DOCS, DOCS))
    row = lax.broadcasted_iota(jnp.int32, (DOCS, DOCS), 0)
    col = lax.broadcasted_iota(jnp.int32, (DOCS, DOCS), 1)
    len_c = jnp.sum(jnp.where(row == col, lens, 0.0), axis=1, keepdims=True)
    end_c = jnp.sum(jnp.where(col <= row, lens, 0.0), axis=1, keepdims=True)
    start_c = end_c - len_c
    base = (ctx * TOK).astype(F32)

    def inside(lo, hi, pos):
        return (lo <= pos) & (pos < hi)

    sel_first = inside(start_c, end_c, base)
    sel_last = inside(start_c, end_c, base + (TOK - 1))

    expert = lax.broadcasted_iota(jnp.int32, (E, TCH), 0).astype(F32)

    def choose(t):
        cols = pl.ds(pl.multiple_of(t * TCH, TCH), TCH)
        own = ids[:, cols].astype(F32)
        miss = own[0:1] - expert
        for k in range(1, K):
            miss = miss * (own[k : k + 1] - expert)
        picked[cols, :] = jnp.where(miss == 0.0, 1.0, 0.0).T

    loop(NTCH, choose)

    loc[...] = jnp.zeros_like(loc)

    def forward(t, logits):
        rows = pl.ds(pl.multiple_of(jnp.maximum(t, 0) * TCH, TCH), TCH)
        aff = sigmoid(logits)
        total = jnp.sum(aff, axis=-1, keepdims=True)
        sh = aff * (1.0 / total)
        share[rows, :] = sh
        coef[rows, :] = (float(E) * sh) * (1.0 - aff)
        chosen = picked[rows, :] * aff
        gate = chosen * (1.0 / jnp.sum(chosen, axis=-1, keepdims=True))
        origin = jnp.where(t < 0, -4.0 * LENGTH, base + (t * TCH).astype(F32))
        pos = lax.broadcasted_iota(jnp.int32, (DOCS, TCH), 1).astype(F32) + origin
        mem = jnp.where(inside(start_c, end_c, pos), 1.0, 0.0).astype(BF16)
        loc[...] += dot(mem, jnp.concatenate(split2(gate), axis=1))

    wcopy.wait()

    def ahead(t, logits):
        xcopy(t).wait()
        rows = pl.ds(pl.multiple_of(t * TCH, TCH), TCH)
        new = dot(xs[rows, :], ws[...])
        forward(t - 1, logits)
        return new

    logits = lax.fori_loop(0, NTCH, ahead, jnp.zeros((TCH, E), F32))
    forward(jnp.int32(NTCH - 1), logits)
    local = loc[:, :E] + loc[:, E:]

    first = jnp.sum(jnp.where(sel_first, local, 0.0), axis=0, keepdims=True)
    last = jnp.sum(jnp.where(sel_last, local, 0.0), axis=0, keepdims=True)
    tile = jnp.concatenate([first[:, :128], first[:, 128:], last[:, :128], last[:, 128:]], axis=0)
    msg[...] = tile
    gat[pl.ds(ctx, 1)] = tile[None]

    pl.semaphore_wait(barrier, NPEER + len(others))

    def spread(src, dst, ssem, rsem):
        peers(lambda n: remote(src, dst.at[ctx], ssem, rsem, peer(n)).start())

    def everyones(dst, ssem, rsem):
        part = dst.at[pl.ds(0, NPEER)]
        return remote(part, part, ssem, rsem, at(dc=1))

    spread(msg, gat, gss, grs)

    row2 = lax.broadcasted_iota(jnp.int32, (DOCS, 2 * DOCS), 0)
    col2 = lax.broadcasted_iota(jnp.int32, (DOCS, 2 * DOCS), 1) % DOCS
    end_r = jnp.sum(jnp.where(row2 <= col2, len_c, 0.0), axis=0, keepdims=True)
    start_r = jnp.sum(jnp.where(row2 < col2, len_c, 0.0), axis=0, keepdims=True)

    def documents(t):
        rows = pl.ds(pl.multiple_of(t * TCH, TCH), TCH)
        pos = lax.broadcasted_iota(jnp.int32, (TCH, 2 * DOCS), 0).astype(F32) + (base + (t * TCH).astype(F32))
        member2[rows, :] = jnp.where(inside(start_r, end_r, pos), 1.0, 0.0).astype(BF16)

    loop(NTCH, documents)

    gcol = lax.broadcasted_iota(jnp.int32, (2 * DOCS, 8 * CTX), 1)
    grow = lax.broadcasted_iota(jnp.int32, (2 * DOCS, 8 * CTX), 0)
    kind = gcol % 8
    gpos = ((gcol // 8) * TOK).astype(F32)
    start2 = jnp.concatenate([start_c, start_c], axis=0)
    end2 = jnp.concatenate([end_c, end_c], axis=0)
    half = grow // DOCS
    s_first = (kind == half) & inside(start2, end2, gpos)
    s_last = (kind == half + 2) & inside(start2, end2, gpos + (TOK - 1)) & (start2 > gpos)
    smat = jnp.where(s_first | s_last, 1.0, 0.0).astype(BF16)

    everyones(gat, gss, grs).wait_recv()
    ghi, glo = split2(jnp.concatenate([gat[...], jnp.zeros((CTX, 4, 128), F32)], axis=1).reshape(8 * CTX, 128))
    sums = dot(smat, jnp.concatenate([ghi, glo], axis=1))
    sums = sums[:, :128] + sums[:, 128:]
    counts = jnp.concatenate([sums[:DOCS], sums[DOCS:]], axis=1)
    counts = counts + jnp.where(sel_first | sel_last, 0.0, local)
    rates = counts * float(E) / len_c
    rates2 = jnp.concatenate(split2(rates), axis=0)

    def backward(t, gsum):
        rows = pl.ds(pl.multiple_of(t * GCH, GCH), GCH)
        tr = dot(member2[rows, :], rates2)
        mean = jnp.sum(tr * share[rows, :], axis=-1, keepdims=True)
        g = coef[rows, :] * (tr - mean)
        grad_out[rows, :] = g
        gbf[rows, :] = g.astype(BF16)
        return gsum + jnp.sum(mean, axis=0, keepdims=True)

    gsum = lax.fori_loop(0, TOK // GCH, backward, jnp.zeros((1, 1), F32))
    btile = jnp.broadcast_to(gsum, (1, 128))
    bmsg[...] = btile
    bgat[pl.ds(ctx, 1)] = btile[None]

    def ahead_z(q):
        return lax.rem(2 + 3 * q + 3 * lax.div(q, 2) + 2 * lax.div(q, 3), 4)

    other = 1 - lax.div(x, 2)

    def core_copy(i):
        return remote(dw.at[i, :, 1 - c], crecv.at[i], css.at[i], crs.at[i], at(dc=1))

    def second(i):
        zq = lax.rem(z + ahead_z(lax.div(i, 2)), 4)
        off = pl.multiple_of(zq * (2 * CHUNK) + lax.rem(other + i, 2) * CHUNK, 128)
        prod = lax.dot_general(
            xs[:, pl.ds(off, CHUNK)], gbf[...], (((0,), (0,)), ((), ())), preferred_element_type=F32
        )
        dw[i] = prod.reshape(2, 2, 4 * ROWS, E)
        core_copy(i).start()

    def core_sum(i):
        core_copy(i).wait_recv()
        q = lax.div(i, 2)
        for xi in range(2):
            xd = 2 * lax.rem(other + i, 2) + xi
            v = (dw[i, xi, pl.ds(c, 1)][0] + crecv[i, xi]).reshape(4, ROWS, E)
            pa[q, xd] = v[:, :RA, :128]
            for yd in range(4):
                pb[q, yd, xd] = v[yd, :RA, 128:]
            pc[q, xd] = v[:, RA:, :]

    H0, H1 = pl.ds(0, 2), pl.ds(2, 2)

    def ring(part, q, kind):
        p, rl, r, near = (pa, arl, ar1, nx) if part == 0 else (pb, brl, br1, ny)
        step = 1 if kind % 2 == 0 else 3
        where = at(dx=step) if part == 0 else at(dy=step)
        opposite, side = near[2], near[step]
        src, dst = (
            (p.at[q, opposite, H0], rl.at[q, 0]),
            (p.at[q, opposite, H1], rl.at[q, 1]),
            (p.at[q, side, H1], r.at[q, 0, H1]),
            (p.at[q, side, H0], r.at[q, 1, H0]),
            (p.at[q, side, H0], r.at[q, 0, H0]),
            (p.at[q, side, H1], r.at[q, 1, H1]),
        )[kind]
        return remote(src, dst, s1.at[part, q, kind], r1.at[part, q, kind], where)

    def ring_z(kind):
        src, dst = (
            (pc.at[0, H0], crl.at[0]),
            (pc.at[0, H1], crl.at[1]),
            (pc.at[1, H1], cr1.at[0, H1]),
            (pc.at[2, H0], cr1.at[1, H0]),
            (pc.at[1, H0], cr1.at[0, H0]),
            (pc.at[2, H1], cr1.at[1, H1]),
        )[kind]
        return remote(src, dst, sz.at[kind], rz.at[kind], at(dz=1 if kind % 2 == 0 else 3))

    def p1(i):
        q = lax.div(i, 2)
        half = lax.rem(other + i, 2)

        @pl.when(half == 0)
        def _():
            @pl.when(q == 0)
            def _():
                ring_z(0).start()

            @pl.when(q == 2)
            def _():
                ring_z(3).start()

            ring(1, q, 0).start()
            ring(1, q, 3).start()

        @pl.when(half == 1)
        def _():
            @pl.when(q == 0)
            def _():
                ring_z(1).start()

            @pl.when(q == 1)
            def _():
                ring_z(2).start()

            ring(1, q, 1).start()
            ring(1, q, 2).start()

        @pl.when(lax.rem(i, 2) == 0)
        def _():
            ring(0, q, 0).start()
            ring(0, q, 1).start()

        @pl.when(lax.rem(x + i, 2) == 0)
        def _():
            ring(0, q, 3).start()

        @pl.when(lax.rem(x + i, 2) == 1)
        def _():
            ring(0, q, 2).start()

    def p2(q):
        for part in range(2):
            p, rl, near = ((pa, arl, nx), (pb, brl, ny))[part]
            for d, (step, h) in enumerate(((1, H0), (3, H1))):
                ring(part, q, d).wait_recv()
                side = near[step]
                p[q, pl.ds(side, 1), h] = p[q, pl.ds(side, 1), h] + rl[q, pl.ds(d, 1)]
                ring(part, q, 4 + d).start()

    def p2_z():
        ring_z(0).wait_recv()
        pc[1, H0] = pc[1, H0] + crl[0]
        ring_z(4).start()
        ring_z(1).wait_recv()
        pc[2, H1] = pc[2, H1] + crl[1]
        ring_z(5).start()

    def a2(q, k):
        return remote(sa.at[q, ny[OFFS[k]]], ar2.at[q, k], s2.at[0, q, k], r2.at[0, q, k], at(dy=OFFS[k]))

    def b2(q):
        q = jnp.int32(q)
        return remote(sb.at[q], br2.at[q], s2.at[1, q, 0], r2.at[1, q, 0], at(dz=ahead_z(q)))

    def c2(k):
        n = 1 + lax.rem(k + 9, 15)
        dx, dy = lax.div(n, 4), lax.rem(n, 4)
        return remote(sc.at[along(nx, dx), along(ny, dy)], cr2.at[n - 1], s2.at[1, 3, 0], r2.at[1, 3, 0], at(dx=dx, dy=dy))

    def c2_all():
        part = cr2.at[pl.ds(0, 15)]
        return remote(part, part, s2.at[1, 3, 0], r2.at[1, 3, 0], at(dc=1))

    def a23(k):
        return remote(sa.at[2, ny[k]], ar4.at[k], s4.at[0, k], r4.at[0, k], at(dz=3, dy=k))

    def b23(k):
        return remote(sb.at[2, nx[k]], br4.at[k], s4.at[1, k], r4.at[1, k], at(dz=3, dx=k))

    def a3(q):
        q = jnp.int32(q)
        return remote(ta.at[q], ar3.at[q], s3.at[0, q], r3.at[0, q], at(dz=ahead_z(q)))

    def b3(k):
        return remote(tb.at[nx[OFFS[k]]], br3.at[k], s3.at[1, k], r3.at[1, k], at(dx=OFFS[k]))

    def p3(q):
        for kind in range(2, 6):
            ring(0, q, kind).wait_recv()
        sa[q] = pa[q, pl.ds(x, 1)][0] + ar1[q, 0] + ar1[q, 1]

        @pl.when(q == 2)
        def _():
            for k in (2, 1, 3, 0):
                a23(k).start()

        @pl.when(q != 2)
        def _():
            for k in range(3):
                a2(q, k).start()

        for kind in range(2, 6):
            ring(1, q, kind).wait_recv()
        sb[q] = pb[q, pl.ds(y, 1)][0] + br1[q, 0] + br1[q, 1]

        @pl.when(q < 2)
        def _():
            b2(q).start()

        @pl.when(q == 2)
        def _():
            for k in (2, 1, 3, 0):
                b23(k).start()

        for kind in range(4):
            ring(0, q, kind).wait_send()
            ring(1, q, kind).wait_send()

    def p4(q):
        for k in range(3):
            a2(q, k).wait_recv()
        ta[q] = sa[q, pl.ds(y, 1)][0] + ar2[q, 0] + ar2[q, 1] + ar2[q, 2]

        @pl.when(q < 2)
        def _():
            a3(q).start()

    def slot(i):
        @pl.when(i < 8)
        def _():
            second(i)

        @pl.when((i >= 2) & (i < 10))
        def _():
            core_sum(i - 2)
            p1(i - 2)

        @pl.when(i == 10)
        def _():
            spread(bmsg, bgat, bss, brs)

        @pl.when((i >= 5) & (i < 12) & (lax.rem(i, 2) == 1))
        def _():
            p2(lax.div(i - 5, 2))

        @pl.when((i >= 9) & (i < 11))
        def _():
            p3(i - 9)

        @pl.when(i == 7)
        def _():
            p2_z()

        @pl.when(i == 11)
        def _():
            for kind in range(2, 6):
                ring_z(kind).wait_recv()
            sc[...] = pc[3] + cr1[0] + cr1[1]
            loop(15, lambda k: c2(k).start())

        @pl.when((i >= 11) & (i < 13))
        def _():
            p3(i - 9)

        @pl.when(i == 12)
        def _():
            for q in range(2):
                b2(q).wait_recv()
            tb[...] = sb[3] + br2[0] + br2[1]
            for k in range(3):
                b3(k).start()

        @pl.when(i >= 11)
        def _():
            p4(i - 11 + lax.div(i, 13))

    loop(14, slot)

    everyones(bgat, bss, brs).wait_recv()
    bal = jnp.sum(bgat[...], axis=0) * (1.0 / LENGTH)
    bal_ref[0] = bal[0, 0]
    loop(8, lambda i: core_copy(i).wait_send())
    everyones(gat, gss, grs).wait_send()
    everyones(bgat, bss, brs).wait_send()
    for kind in range(6):
        ring_z(kind).wait_send()

    def ring_sent(q):
        for kind in range(4, 6):
            ring(0, q, kind).wait_send()
            ring(1, q, kind).wait_send()

    loop(4, ring_sent)
    scale = 1.0 / math.sqrt(LENGTH * 4)
    c2_all().wait_recv()
    own_c = sc[pl.ds(x, 1), pl.ds(y, 1)].reshape(RC, E)
    wg_ref[RA:, :] = (own_c + jnp.sum(cr2[...], axis=0)) * scale
    for k in range(2):
        a3(k).wait_recv()
    for k in range(4):
        a23(k).wait_recv()
    wg_ref[:RA, :128] = (ta[3] + ar3[0] + ar3[1] + ((ar4[0] + ar4[1]) + (ar4[2] + ar4[3]))) * scale
    for k in range(4):
        b23(k).wait_recv()
    for k in range(3):
        b3(k).wait_recv()
    own_b = tb[pl.ds(x, 1)][0] + br3[0] + br3[1] + br3[2]
    wg_ref[:RA, 128:] = (own_b + ((br4[0] + br4[1]) + (br4[2] + br4[3]))) * scale
    for k in range(3):
        for q in (0, 1, 3):
            a2(q, k).wait_send()
        b3(k).wait_send()
    for k in range(2):
        b2(k).wait_send()
        a3(k).wait_send()
    for k in range(4):
        a23(k).wait_send()
        b23(k).wait_send()
    c2_all().wait_send()


def scratch():
    v = pltpu.VMEM
    s = pltpu.SemaphoreType.DMA
    return [
        v((K, TOK), jnp.int32), v((1, DOCS), jnp.int32),
        v((TOK, D), BF16), v((D, E), BF16), v((TOK, E), F32), v((TOK, E), F32), v((TOK, E), F32),
        v((TOK, E), BF16), v((DOCS, 2 * E), F32),
        v((8, 2, 2, 4 * ROWS, E), F32), v((8, 2, 4 * ROWS, E), F32),
        v((4, 4, 4, RA, 128), F32), v((4, 4, 4, RA, 128), F32), v((4, 4, 4, RC, E), F32),
        v((4, 2, 2, RA, 128), F32), v((4, 2, 2, RA, 128), F32), v((2, 2, 4, RC, E), F32),
        v((4, 2, 4, RA, 128), F32), v((4, 2, 4, RA, 128), F32), v((2, 4, 4, RC, E), F32),
        v((4, 4, RA, 128), F32), v((4, 4, RA, 128), F32), v((4, 4, RC, E), F32),
        v((4, 3, RA, 128), F32), v((2, 4, RA, 128), F32), v((15, RC, E), F32),
        v((4, RA, 128), F32), v((4, RA, 128), F32),
        v((2, RA, 128), F32), v((3, RA, 128), F32), v((4, RA, 128), F32), v((4, RA, 128), F32),
        v((4, 128), F32), v((CTX, 4, 128), F32), v((1, 128), F32), v((CTX, 1, 128), F32), v((TOK, 2 * DOCS), BF16),
        s((2,)), s((NTCH,)), s, s, s, s, s, s((8,)), s((8,)),
        s((2, 4, 6)), s((2, 4, 6)), s((6,)), s((6,)), s((2, 4, 3)), s((2, 4, 3)), s((3, 3)), s((3, 3)), s((2, 4)), s((2, 4)),
    ]


def shards(hidden, router_weight, expert_ids, doc_lengths):
    vm = pl.BlockSpec(memory_space=pltpu.VMEM)
    hbm = pl.BlockSpec(memory_space=pl.ANY)
    balance, grad, weight_grad = pl.pallas_call(
        kernel,
        out_shape=(
            pltpu.SMEM((1,), F32),
            pltpu.VMEM((TOK, E), F32),
            pltpu.VMEM((ROWS, E), F32),
        ),
        in_specs=[hbm, hbm, hbm, hbm],
        out_specs=(pl.BlockSpec(memory_space=pltpu.SMEM), vm, vm),
        scratch_shapes=scratch(),
        compiler_params=pltpu.CompilerParams(
            collective_id=0, has_side_effects=True, vmem_limit_bytes=60 << 20
        ),
        name="balance_loss",
    )(hidden[0], router_weight, expert_ids[0].T, doc_lengths)
    return balance, grad[None], weight_grad


def solution(mesh):
    placed = (P("win", "ctx", None), P(), P("win", "ctx", None), P("win", None))
    return jax.shard_map(
        shards,
        mesh=mesh,
        in_specs=placed,
        out_specs=(P("win"), P("win", "ctx", None), P(("ctx", "win"), None)),
        check_vma=False,
    )
```
